32 devices in a mesh: blk: 4 (over y, x), batch: 8 (over z, core).
Axes of the slice: x: 2, y: 2, z: 4, core: 2. Of those that a mesh axis runs over, the one named last changes fastest.
Arguments:
- hidden_in: bfloat16 [48, 1024, 576], P('batch', 'blk'), may hold values from -6 to 6
- lengths: int32 [48], P('batch'), may hold values from 256 to 1024, as said below
- attn_gain: bfloat16 [576], replicated, may hold values from 0.099609375 to 1.8984375
- w_query: bfloat16 [576, 576], replicated, may hold values from -0.25 to 0.25
- w_key: bfloat16 [576, 192], replicated, may hold values from -0.25 to 0.25
- w_value: bfloat16 [576, 192], replicated, may hold values from -0.25 to 0.25
- w_output: bfloat16 [576, 576], replicated, may hold values from -3 to 3
- mlp_gain: bfloat16 [576], replicated, may hold values from 0.099609375 to 1.8984375
- w_gate: bfloat16 [576, 1536], replicated, may hold values from -0.25 to 0.25
- w_up: bfloat16 [576, 1536], replicated, may hold values from -0.25 to 0.25
- w_down: bfloat16 [1536, 576], replicated, may hold values from -0.15625 to 0.15625
- cotangent: bfloat16 [48, 1024, 576], P('batch', 'blk'), may hold values from -6 to 6
Outputs:
- layer_out: bfloat16 [48, 1024, 576], P('batch', 'blk')
- grad_in: bfloat16 [48, 1024, 576], P('batch', 'blk')
- grad_attn_gain: float32 [576], replicated
- grad_w_query: float32 [576, 576], replicated
- grad_w_key: float32 [576, 192], replicated
- grad_w_value: float32 [576, 192], replicated
- grad_w_output: float32 [576, 576], replicated
- grad_mlp_gain: float32 [576], replicated
- grad_w_gate: float32 [576, 1536], replicated
- grad_w_up: float32 [576, 1536], replicated
- grad_w_down: float32 [1536, 576], replicated
The draws below stay inside these ranges and needn't reach their ends.
Inputs may be any that keep to these rules, and one draw needn't show every extreme that they name: `lengths`: each sequence holds its tokens in slots 0 to length - 1; in each group of 6 sequences that share an index of batch, one fills all 1024 slots.
All inputs are finite; a program needn't handle non-finite values.
Results may differ from the reference program's by a relative error of at most 0.018.
Values may be sent and summed in bfloat16 or wider, within the bound.
No kernel may reach another device: no remote copies, remote signals or barrier semaphores. Data moves between devices by JAX's collectives and lax.ppermute only.
A program may use at most 256 MiB of HBM per device.

```python
import jax
import jax.numpy as jnp
from jax import lax

D = 576
HEADS = 9
KV_HEADS = 3
HEAD_DIM = 64
FF = 1536
SEQ_DEV = 6
MIN_LEN = 256
SLOTS = 1024
SEQS = 48


def draw_lengths(key, part):
    key = jax.random.fold_in(key, 11)
    base_key, pick_key = jax.random.split(key)
    group_count = SEQS // SEQ_DEV
    drawn = jax.random.randint(base_key, (SEQS,), MIN_LEN, SLOTS + 1, dtype=jnp.int32)
    picked = jax.random.randint(pick_key, (group_count,), 0, SEQ_DEV, dtype=jnp.int32)
    chosen = jnp.arange(group_count, dtype=jnp.int32) * SEQ_DEV + picked
    filled = jnp.any(jnp.arange(SEQS, dtype=jnp.int32)[:, None] == chosen[None, :], axis=1)
    return jnp.where(filled, SLOTS, drawn).astype(jnp.int32)


def levels(rng, shape, cuts, low, largest):
    def one(dim, parts):
        draws = jax.random.uniform(jax.random.fold_in(jax.random.fold_in(rng, 6), dim), (parts,), jnp.float32, low / len(cuts), largest / len(cuts))
        return jnp.repeat(jnp.exp(draws), shape[dim] // parts).reshape((-1,) + (1,) * (len(shape) - dim - 1))

    factor_of = one(*cuts[0])
    for cut in cuts[1:]:
        factor_of = factor_of * one(*cut)
    return factor_of


def normal_values(key, extent, spread, bound, cuts=(), kind=jnp.bfloat16):
    level = levels(key, extent, cuts, -0.22, 0.18) if cuts else 1.0
    values = jax.random.normal(key, extent, jnp.float32) * spread * level
    return jnp.minimum(jnp.maximum(values, -bound), bound).astype(kind)


def setup_inputs(seed: int = 0) -> dict:
    splits = jax.random.split(jax.random.key(seed), 13)
    return {
        "hidden_in": normal_values(splits[0], (SEQS, SLOTS, D), 1.0, 6.0, ((0, 8), (1, 4))),
        "lengths": draw_lengths(jax.random.fold_in(splits[12], 71), 0),
        "attn_gain": jnp.clip(1.0 + 0.18 * jax.random.normal(splits[2], (D,), jnp.float32), 0.099609375, 1.8984375).astype(jnp.bfloat16),
        "w_query": normal_values(splits[3], (D, HEADS * HEAD_DIM), D ** -0.5, 0.25),
        "w_key": normal_values(splits[4], (D, KV_HEADS * HEAD_DIM), D ** -0.5, 0.25),
        "w_value": normal_values(splits[5], (D, KV_HEADS * HEAD_DIM), D ** -0.5, 0.25),
        "w_output": normal_values(splits[6], (HEADS * HEAD_DIM, D), 4 ** -0.5, 3.0),
        "mlp_gain": jnp.clip(1.0 + 0.18 * jax.random.normal(splits[7], (D,), jnp.float32), 0.099609375, 1.8984375).astype(jnp.bfloat16),
        "w_gate": normal_values(splits[8], (D, FF), D ** -0.5, 0.25),
        "w_up": normal_values(splits[9], (D, FF), D ** -0.5, 0.25),
        "w_down": normal_values(splits[10], (FF, D), FF ** -0.5, 0.15625),
        "cotangent": normal_values(splits[11], (SEQS, SLOTS, D), 1.0, 6.0, ((0, 8), (1, 4))),
    }


EPS = 1e-05
THETA = 10000.0
NEGATIVE = -1e+30
HIGH = lax.Precision.HIGHEST

@jax.custom_vjp
def low(v):
    return lax.optimization_barrier(v.astype(jnp.bfloat16)).astype(jnp.float32)

@jax.custom_vjp
def low_back(v):
    return v

def low_keep(v):
    return (low(v), None)

def low_pass(kept, grad):
    return (grad,)

def back_keep(v):
    return (v, None)

def back_low(kept, grad):
    return (low(grad),)
low.defvjp(low_keep, low_pass)
low_back.defvjp(back_keep, back_low)

def rope_table(count):
    half_dim = HEAD_DIM // 2
    frequency = THETA ** (-jnp.arange(half_dim, dtype=jnp.float32) * 2.0 / HEAD_DIM)
    places = jnp.arange(count, dtype=jnp.int32).astype(jnp.float32)
    angles = places[:, None] * frequency[None, :]
    return (jnp.cos(angles), jnp.sin(angles))

def rotate(values, cos_table, sin_table):
    half_dim = values.shape[-1] // 2
    leading = values[..., :half_dim]
    trailing = values[..., half_dim:]
    cos_wide = cos_table[:, None, :]
    sin_wide = sin_table[:, None, :]
    return jnp.concatenate([leading * cos_wide - trailing * sin_wide, trailing * cos_wide + leading * sin_wide], -1)

def rms_norm(inputs, gain):
    return inputs * lax.rsqrt(lax.optimization_barrier(jnp.mean(inputs * inputs, -1, keepdims=True)) + EPS) * gain

def layer_sequence(params, inputs, length):
    attn_gain, w_query, w_key, w_value, w_output, mlp_gain, w_gate, w_up, w_down = params
    slot_count = inputs.shape[0]
    groups = HEADS // KV_HEADS
    cos_table, sin_table = rope_table(slot_count)
    normed = low(rms_norm(inputs, attn_gain))
    query_lin = low_back(jnp.dot(normed, w_query, precision=HIGH)).reshape(slot_count, HEADS, HEAD_DIM)
    key_lin = low_back(jnp.dot(normed, w_key, precision=HIGH)).reshape(slot_count, KV_HEADS, HEAD_DIM)
    values = low(low_back(jnp.dot(normed, w_value, precision=HIGH))).reshape(slot_count, KV_HEADS, HEAD_DIM)
    queries = low(rotate(query_lin, cos_table, sin_table)).reshape(slot_count, KV_HEADS, groups, HEAD_DIM)
    keys = low(rotate(key_lin, cos_table, sin_table))
    scores = jnp.einsum('qkgd,pkd->kgqp', queries, keys, precision=HIGH) * HEAD_DIM ** (-0.5)
    scores = low_back(scores)
    places = jnp.arange(slot_count, dtype=jnp.int32)
    allowed = (places[None, :] <= places[:, None]) & (places[None, :] < length)
    scores = jnp.where(allowed, scores, NEGATIVE)
    probs_low = low(jax.nn.softmax(scores, axis=-1))
    attn_mix = jnp.einsum('kgqp,pkd->qkgd', probs_low, values, precision=HIGH).reshape(slot_count, HEADS * HEAD_DIM)
    attn_mix = low(low_back(attn_mix))
    middle = inputs + low_back(jnp.dot(attn_mix, w_output, precision=HIGH))
    normed2 = low(rms_norm(middle, mlp_gain))
    gate = low_back(jnp.dot(normed2, w_gate, precision=HIGH))
    up_part = low_back(jnp.dot(normed2, w_up, precision=HIGH))
    hidden = low(jax.nn.silu(gate) * up_part)
    branch = low_back(jnp.dot(hidden, w_down, precision=HIGH))
    valid = (places < length).astype(inputs.dtype)[:, None]
    return valid * (middle + branch)

def reference(hidden_in, lengths, attn_gain, w_query, w_key, w_value, w_output, mlp_gain, w_gate, w_up, w_down, cotangent):
    params = tuple((weight.astype(jnp.float32) for weight in (attn_gain, w_query, w_key, w_value, w_output, mlp_gain, w_gate, w_up, w_down)))
    inputs = hidden_in.astype(jnp.float32)

    def forward(params, inputs):

        def one_sequence(members):
            return layer_sequence(params, members[0], members[1])
        return lax.map(jax.checkpoint(one_sequence), (inputs, lengths))
    outputs, pullback = jax.vjp(forward, params, inputs)
    grads, grad_inputs = pullback(cotangent.astype(jnp.float32))
    return (outputs.astype(jnp.bfloat16), grad_inputs.astype(jnp.bfloat16), grads[0], grads[1], grads[2], grads[3], grads[4], grads[5], grads[6], grads[7], grads[8])
```

```python
import functools

import jax
import jax.numpy as jnp
import numpy as np
from jax import lax
from jax.experimental import pallas as pl
from jax.experimental.pallas import tpu as pltpu
from jax.sharding import PartitionSpec as P

HEADS = 9
KV_HEADS = 3
HEAD_DIM = 64
GROUPS = HEADS // KV_HEADS
HALF = HEAD_DIM // 2
KV_WIDTH = KV_HEADS * HEAD_DIM
Q_WIDTH = HEADS * HEAD_DIM

EPS = 1e-05
THETA = 10000.0
NEGATIVE = -1e30
LANES = 128
F32 = jnp.float32
BF16 = jnp.bfloat16
VMEM_LIMIT = 60 * 1024 * 1024

NN = (((1,), (0,)), ((), ()))
NT = (((1,), (1,)), ((), ()))
TN = (((0,), (0,)), ((), ()))


def dot(a, b, dims=NN):
    return lax.dot_general(a, b, dims, preferred_element_type=F32)


def call(
    kernel, name, grid, in_specs, out_specs, out_shape, scratch=(), flops=0, bytes_accessed=0, after=()
):
    count, more = len(in_specs), len(after)

    def body(info, *refs):
        kernel(info, *refs[:count], *refs[count + more :])

    made = pl.pallas_call(
        body,
        grid_spec=pltpu.PrefetchScalarGridSpec(
            num_scalar_prefetch=1,
            grid=grid,
            in_specs=list(in_specs) + [pl.BlockSpec(memory_space=pl.ANY)] * more,
            out_specs=out_specs,
            scratch_shapes=list(scratch),
        ),
        out_shape=out_shape,
        compiler_params=pltpu.CompilerParams(
            dimension_semantics=("arbitrary",), vmem_limit_bytes=VMEM_LIMIT
        ),
        cost_estimate=pl.CostEstimate(
            flops=int(flops), bytes_accessed=int(bytes_accessed), transcendentals=0
        ),
        name=name,
    )
    return lambda *operands: made(*operands, *after)


def per_step(*shape):
    zeros = (0,) * len(shape)
    return pl.BlockSpec((1,) + shape, lambda s, info: (s,) + zeros)


def whole(*shape):
    zeros = (0,) * len(shape)
    return pl.BlockSpec(shape, lambda s, info: zeros, pipeline_mode=pl.Buffered(1))


def kept(*shape):
    zeros = (0,) * len(shape)
    return pl.BlockSpec(shape, lambda s, info: zeros)


def valid_rows(info, slot, block, positions):
    return jnp.clip(info[slot] - block * positions, 0, positions)


def first_bit(count, slots):
    return slots + 1 + count * slots


def pick(count, info, *refs):
    for distance in range(count):
        refs[count + distance][...] = refs[distance][...]


def put(count, last, info, *refs):
    distance = info[last + pl.program_id(0)]
    for which in range(count):

        @pl.when(distance == which)
        def _():
            refs[count][...] = refs[which][...]


def rotate(lin, cos, sin, heads, store):
    for head in range(heads):
        low = head * HEAD_DIM
        lead, trail = lin[low : low + HALF], lin[low + HALF : low + HEAD_DIM]
        store(low, (lead * cos - trail * sin).astype(BF16))
        store(low + HALF, (trail * cos + lead * sin).astype(BF16))


def front(positions, count, info, *refs):
    x_refs, refs = refs[:count], refs[count:]
    gain_ref, wq_ref, wkv_ref, cos_ref, sin_ref = refs[:5]
    normed_ref, q_ref, kv_ref, mix_ref, log_ref, stat, acc = refs[5:]
    slot = pl.program_id(0)
    blk = info[pl.num_programs(0)]
    blocks = lax.div(info[slot] + positions - 1, positions)

    for distance in range(count):
        block = blk ^ distance

        @pl.when(block < blocks)
        def _():
            x = x_refs[distance][0].astype(F32)
            scaled = lax.rsqrt(jnp.mean(x * x, axis=0, keepdims=True) + EPS)
            normed = (x * scaled * gain_ref[...]).astype(BF16)
            normed_ref[0, block] = normed
            cos, sin = cos_ref[block], sin_ref[block]
            lin = dot(wkv_ref[...], normed)

            def store_kv(low, value):
                kv_ref[0, block, low : low + HALF] = value

            rotate(lin, cos, sin, KV_HEADS, store_kv)
            kv_ref[0, block, KV_WIDTH:] = lin[KV_WIDTH:].astype(BF16)

            def store_q(low, value):
                q_ref[0, block, low : low + HALF] = value

            rotate(dot(wq_ref[...], normed) * (HEAD_DIM**-0.5), cos, sin, HEADS, store_q)

    def visit(block, other, diagonal):
        if diagonal:
            mask = causal_mask(positions, GROUPS)
        for group in range(KV_HEADS):
            low = group * HEAD_DIM
            key = kv_ref[0, other, low : low + HEAD_DIM]
            value = kv_ref[0, other, KV_WIDTH + low : KV_WIDTH + low + HEAD_DIM]
            scores = dot(key, heads_side_by_side(q_ref, block, group), TN)
            if diagonal:
                scores = jnp.where(mask, scores, NEGATIVE)
            peak = jnp.max(scores, axis=0, keepdims=True)
            if not diagonal:
                old = stat[group : group + 1]
                peak = jnp.maximum(peak, old)
            weights = jnp.exp(scores - peak)
            total = jnp.sum(weights, axis=0, keepdims=True)
            summed = dot(value, weights.astype(BF16))
            if not diagonal:
                fade = jnp.exp(old - peak)
                total = total + stat[KV_HEADS + group : KV_HEADS + group + 1] * fade
                summed = summed + acc[low : low + HEAD_DIM] * fade
            stat[group : group + 1] = peak
            stat[KV_HEADS + group : KV_HEADS + group + 1] = total
            acc[low : low + HEAD_DIM] = summed

    def one_block(block, carry):
        visit(block, block, True)

        def one_pair(other, carry):
            visit(block, other, False)
            return carry

        lax.fori_loop(0, block, one_pair, 0)
        log_ref[0, block] = stat[:KV_HEADS] + jnp.log(stat[KV_HEADS:])
        for group in range(KV_HEADS):
            low = group * HEAD_DIM
            share = 1.0 / stat[KV_HEADS + group : KV_HEADS + group + 1]
            mix = (acc[low : low + HEAD_DIM] * share).astype(BF16)
            for place in range(GROUPS):
                row = (group * GROUPS + place) * HEAD_DIM
                mix_ref[0, block, row : row + HEAD_DIM] = mix[
                    :, place * positions : (place + 1) * positions
                ]
        return carry

    lax.fori_loop(0, blocks, one_block, 0)


def causal_mask(positions, copies):
    keys = lax.broadcasted_iota(jnp.int32, (positions, positions), 0)
    queries = lax.broadcasted_iota(jnp.int32, (positions, positions), 1)
    return jnp.concatenate([keys <= queries] * copies, 1)


def heads_side_by_side(ref, block, group):
    first = group * GROUPS * HEAD_DIM
    return jnp.concatenate(
        [ref[0, block, first + p * HEAD_DIM : first + (p + 1) * HEAD_DIM] for p in range(GROUPS)],
        1,
    )


def pieces_of(columns):
    return [(start, min(LANES, columns - start)) for start in range(0, columns, LANES)]


class Parts:
    def __init__(self, halves, count, blk):
        self.halves, self.count, self.blk = halves, count, blk
        self.size = halves[0].shape[0] // count

    def write(self, row, value):
        done, rows = 0, value.shape[0]
        while done < rows:
            part, inside = divmod(row + done, self.size)
            take = min(self.size - inside, rows - done)
            half, part = divmod(part, self.count)
            start = pl.multiple_of((part ^ self.blk) * self.size + inside, 16)
            self.halves[half][pl.ds(start, take)] = value[done : done + take]
            done += take


def pack_into(parts, row, acc):
    rows, columns = acc.shape
    for start, width in pieces_of(columns):
        part = acc[:, start : start + width].astype(BF16)
        if width < LANES:
            half = rows // 2
            part = jnp.concatenate([part[:half], part[half:]], 1)
        parts.write(row, part)
        row += part.shape[0]
    return row


def gain_rows(acc):
    ones = jnp.ones((16, acc.shape[1]), BF16)
    sums = dot(ones, acc[...].astype(BF16), NT)[:1]
    parts = [sums[:, start : start + width] for start, width in pieces_of(sums.shape[1])]
    short = LANES - parts[-1].shape[1]
    if short:
        parts[-1] = jnp.concatenate([parts[-1], jnp.zeros((1, short), F32)], 1)
    return parts


def pack_all(info, bit_at, count, blk, mine_ref, send_ref, accs, last=None):
    def fill(halves):
        parts = Parts(halves, count, blk)
        row = 0
        for acc in accs:
            row = pack_into(parts, row, acc)
        if last is not None:
            parts.write(row, last)
            row += last.shape[0]
        rest = 2 * mine_ref.shape[0] - row
        if rest:
            parts.write(row, jnp.zeros((rest, LANES), BF16))

    pl.when(info[bit_at] == 0)(lambda: fill((mine_ref, send_ref)))
    pl.when(info[bit_at] != 0)(lambda: fill((send_ref, mine_ref)))


def packed_rows(rows, columns):
    return rows * columns // LANES


def feed_forward(
    positions,
    chunk,
    count,
    slots,
    info,
    *refs,
):
    x_refs, cot_refs, refs = refs[:count], refs[count : 2 * count], refs[2 * count :]
    ins, out_refs, rest = refs[:10], refs[10 : 10 + count], refs[10 + count :]
    feed_forward_step(
        positions, chunk, count, slots, info, x_refs, cot_refs, out_refs, *ins, *rest
    )


def feed_forward_step(
    positions,
    chunk,
    count,
    slots,
    info,
    x_refs,
    cot_refs,
    out_refs,
    mix_ref,
    gain_ref,
    wo_t_ref,
    wo_ref,
    wg_t_ref,
    wg_ref,
    wu_t_ref,
    wu_ref,
    wd_t_ref,
    wd_ref,
    mid_ref,
    gattn_ref,
    delta_ref,
    mine_ref,
    send_ref,
    gain_sum_ref,
    acc_gate,
    acc_up,
    acc_down,
    acc_out,
    x_now,
    cot_now,
    out_now,
):
    step = pl.program_id(0)
    distance, slot = lax.div(step, slots), lax.rem(step, slots)
    rows = valid_rows(info, slot, info[slots] ^ distance, positions)
    width = x_now.shape[0]
    hidden_width = wg_ref.shape[1]

    @pl.when(step == 0)
    def _():
        acc_gate[...] = jnp.zeros_like(acc_gate)
        acc_up[...] = jnp.zeros_like(acc_up)
        acc_down[...] = jnp.zeros_like(acc_down)
        acc_out[...] = jnp.zeros_like(acc_out)
        gain_sum_ref[...] = jnp.zeros_like(gain_sum_ref)

    @pl.when(rows <= 0)
    def _():
        out_now[...] = jnp.zeros_like(out_now)

    for which in range(count):

        @pl.when(jnp.logical_and(rows > 0, distance == which))
        def _():
            x_now[...] = x_refs[which][0]
            cot_now[...] = cot_refs[which][0]

    @pl.when(rows > 0)
    def _():
        lane = lax.broadcasted_iota(jnp.int32, (1, positions), 1)
        valid = (lane < rows).astype(F32)
        mix = mix_ref[0, 0]
        middle = x_now[...].astype(F32) + dot(wo_t_ref[...], mix)
        scaled = lax.rsqrt(jnp.mean(middle * middle, axis=0, keepdims=True) + EPS)
        normal = middle * scaled
        gain = gain_ref[...]
        normed = (normal * gain).astype(BF16)
        grad_y = cot_now[...].astype(F32) * valid
        grad_low = grad_y.astype(BF16)
        branch = jnp.zeros((width, positions), F32)
        grad_normed = jnp.zeros((width, positions), F32)
        for start in range(0, hidden_width, chunk):
            part = slice(start, start + chunk)
            gate = dot(wg_t_ref[part], normed)
            up = dot(wu_t_ref[part], normed)
            grad_hidden = dot(wd_ref[part], grad_low)
            sig = 1.0 / (1.0 + jnp.exp(-gate))
            act = gate * sig
            hidden = (act * up).astype(BF16)
            grad_gate = (grad_hidden * up * (sig * (1.0 + gate * (1.0 - sig)))).astype(BF16)
            grad_up = (grad_hidden * act).astype(BF16)
            branch = branch + dot(wd_t_ref[:, part], hidden)
            grad_normed = grad_normed + dot(wg_ref[:, part], grad_gate)
            grad_normed = grad_normed + dot(wu_ref[:, part], grad_up)
            acc_down[:, part] += dot(grad_low, hidden, NT)
            acc_gate[:, part] += dot(normed, grad_gate, NT)
            acc_up[:, part] += dot(normed, grad_up, NT)
        out_now[...] = (valid * (middle + branch)).astype(BF16)
        gain_sum_ref[...] += grad_normed * normal
        inner = grad_normed * gain
        mean = jnp.mean(inner * normal, axis=0, keepdims=True)
        grad_middle = grad_y + scaled * (inner - normal * mean)
        mid_ref[0, 0] = grad_middle.astype(BF16)
        grad_mid_low = grad_middle.astype(BF16)
        acc_out[...] += dot(mix, grad_mid_low, NT)
        grad_attn = dot(wo_ref[...], grad_mid_low).astype(BF16)
        gattn_ref[0, 0] = grad_attn
        product = grad_attn.astype(F32) * mix.astype(F32)
        for head in range(HEADS):
            part = slice(head * HEAD_DIM, (head + 1) * HEAD_DIM)
            group, place = head // GROUPS, head % GROUPS
            delta_ref[0, 0, group : group + 1, place * positions : (place + 1) * positions] = jnp.sum(
                product[part], axis=0, keepdims=True
            )

    for which in range(count):

        @pl.when(distance == which)
        def _():
            out_refs[which][0] = out_now[...]

    @pl.when(step == count * slots - 1)
    def _():
        pack_all(
            info,
            first_bit(count, slots),
            count,
            info[slots],
            mine_ref,
            send_ref,
            (acc_gate, acc_up, acc_down, acc_out),
        )


def rotate_back(value, cos, sin, heads):
    parts = []
    for head in range(heads):
        low = head * HEAD_DIM
        lead, trail = value[low : low + HALF], value[low + HALF : low + HEAD_DIM]
        parts += [lead * cos + trail * sin, trail * cos - lead * sin]
    return jnp.concatenate(parts, 0)


def attend_back(positions, count, info, *refs):
    q_ref, kv_ref, gattn_ref, log_ref, delta_ref, cos_ref, sin_ref = refs[:7]
    lin_ref, dq, dkv = refs[7:]
    blocks = lax.div(info[pl.program_id(0)] + positions - 1, positions)

    def visit(block, other, diagonal):
        if diagonal:
            mask = causal_mask(positions, GROUPS)
        for group in range(KV_HEADS):
            low = group * HEAD_DIM
            key = kv_ref[0, other, low : low + HEAD_DIM]
            value = kv_ref[0, other, KV_WIDTH + low : KV_WIDTH + low + HEAD_DIM]
            query = heads_side_by_side(q_ref, block, group)
            grad = heads_side_by_side(gattn_ref, block, group)
            scores = dot(key, query, TN)
            probs = jnp.exp(scores - log_ref[0, block, group : group + 1])
            if diagonal:
                probs = jnp.where(mask, probs, 0.0)
            grad_probs = dot(value, grad, TN)
            delta = delta_ref[0, block, group : group + 1]
            grad_scores = (probs * (grad_probs - delta)).astype(BF16)
            grad_query = dot(key, grad_scores)
            grad_key = dot(query, grad_scores, NT)
            grad_value = dot(grad, probs.astype(BF16), NT)
            rows = slice(low, low + HEAD_DIM)
            more = slice(KV_WIDTH + low, KV_WIDTH + low + HEAD_DIM)
            if diagonal:
                dq[rows] = grad_query
                dkv[other, rows] = grad_key
                dkv[other, more] = grad_value
            else:
                dq[rows] += grad_query
                dkv[other, rows] += grad_key
                dkv[other, more] += grad_value

    def one_block(block, carry):
        visit(block, block, True)

        def one_pair(other, carry):
            visit(block, other, False)
            return carry

        lax.fori_loop(0, block, one_pair, 0)
        grad = jnp.concatenate(
            [
                dq[
                    (head // GROUPS) * HEAD_DIM : (head // GROUPS + 1) * HEAD_DIM,
                    (head % GROUPS) * positions : (head % GROUPS + 1) * positions,
                ]
                for head in range(HEADS)
            ],
            0,
        ) * (HEAD_DIM**-0.5)
        lin = rotate_back(grad, cos_ref[block], sin_ref[block], HEADS)
        lin_ref[0, block, :Q_WIDTH] = lin.astype(BF16)
        return carry

    lax.fori_loop(0, blocks, one_block, 0)

    def one_rotation(block, carry):
        grad = dkv[block]
        rotated = rotate_back(grad[:KV_WIDTH], cos_ref[block], sin_ref[block], KV_HEADS)
        lin_ref[0, block, Q_WIDTH : Q_WIDTH + KV_WIDTH] = rotated.astype(BF16)
        lin_ref[0, block, Q_WIDTH + KV_WIDTH :] = grad[KV_WIDTH:].astype(BF16)
        return carry

    lax.fori_loop(0, blocks, one_rotation, 0)


def project_back(positions, count, slots, info, *refs):
    x_refs, refs = refs[:count], refs[count:]
    gain_ref, normed_ref, lin_ref, mid_ref, w_ref, other_gain_ref = refs[:6]
    out_refs, refs = refs[6 : 6 + count], refs[6 + count :]
    mine_ref, send_ref, gain_sum, acc_q, acc_k, acc_v, x_now, out_now = refs
    step = pl.program_id(0)
    distance, slot = lax.div(step, slots), lax.rem(step, slots)
    blk = info[slots]
    rows = valid_rows(info, slot, blk ^ distance, positions)

    @pl.when(step == 0)
    def _():
        acc_q[...] = jnp.zeros_like(acc_q)
        acc_k[...] = jnp.zeros_like(acc_k)
        acc_v[...] = jnp.zeros_like(acc_v)
        gain_sum[...] = jnp.zeros_like(gain_sum)

    for which in range(count):

        @pl.when(jnp.logical_and(rows > 0, distance == which))
        def _():
            x_now[...] = x_refs[which][0]

    @pl.when(rows <= 0)
    def _():
        out_now[...] = jnp.zeros_like(out_now)

    @pl.when(rows > 0)
    def _():
        lin = lin_ref[0, 0]
        normed = normed_ref[0, 0]
        acc_q[...] += dot(normed, lin[:Q_WIDTH], NT)
        acc_k[...] += dot(lin[Q_WIDTH : Q_WIDTH + KV_WIDTH], normed, NT)
        acc_v[...] += dot(lin[Q_WIDTH + KV_WIDTH :], normed, NT)
        grad_normed = dot(w_ref[...], lin)
        x = x_now[...].astype(F32)
        scaled = lax.rsqrt(jnp.mean(x * x, axis=0, keepdims=True) + EPS)
        normal = x * scaled
        gain_sum[...] += grad_normed * normal
        inner = grad_normed * gain_ref[...]
        mean = jnp.mean(inner * normal, axis=0, keepdims=True)
        middle = mid_ref[0, 0].astype(F32)
        out_now[...] = (middle + scaled * (inner - normal * mean)).astype(BF16)

    for which in range(count):

        @pl.when(distance == which)
        def _():
            out_refs[which][0] = out_now[...]

    @pl.when(step == count * slots - 1)
    def _():
        gains = gain_rows(gain_sum) + gain_rows(other_gain_ref)
        gains.append(jnp.zeros((-len(gains) % 16, LANES), F32))
        gains = jnp.concatenate(gains, 0).astype(BF16)
        pack_all(
            info,
            first_bit(count, slots),
            count,
            blk,
            mine_ref,
            send_ref,
            (acc_q, acc_k, acc_v),
            gains,
        )


def unpack(count, slots, shapes, gain_width, start, size, info, *refs):
    out_refs, buffer = refs[2 * count : -1], refs[-1]
    core = info[first_bit(count, slots)]
    for which in range(2):
        for distance in range(count):
            part = (core ^ which) * count + (info[slots] ^ distance)
            buffer[pl.ds(pl.multiple_of(part * size, 16), size)] = refs[which * count + distance][
                start : start + size
            ]
    row = 0
    for ref, (rows, columns) in zip(out_refs, shapes):
        for first, width in pieces_of(columns):
            if width == LANES:
                ref[:, first : first + LANES] = buffer[row : row + rows].astype(F32)
                row += rows
            else:
                half = rows // 2
                part = buffer[row : row + half].astype(F32)
                ref[:half, first : first + width] = part[:, :width]
                ref[half:, first : first + width] = part[:, width:]
                row += half
    if gain_width:
        gains = buffer[row : row + 16].astype(F32)
        line = 0
        for ref in out_refs[len(shapes) :]:
            for first, width in pieces_of(gain_width):
                ref[:, first : first + width] = gains[line : line + 1, :width]
                line += 1


def line_up(count, at, info, *refs):
    size = refs[0].shape[0]
    for distance in range(count):
        start = pl.multiple_of((info[at] ^ distance) * size, 16)
        refs[count][pl.ds(start, size)] = refs[distance][...]


def added(arrays):
    total = arrays[0].astype(F32)
    for array in arrays[1:]:
        total = total + array.astype(F32)
    return total.astype(BF16)


class Sum:
    def __init__(self, blk_count, batch_count):
        self.blk_count, self.rest_count = blk_count, batch_count // 2
        self.rest = lax.axis_index("batch") // 2

    def swap_cores(self, array):
        pairs = [(i, i ^ 1) for i in range(2 * self.rest_count)]
        return lax.ppermute(array, "batch", pairs)

    def over_blk(self, array, distance):
        return lax.ppermute(array, "blk", [(i, i ^ distance) for i in range(self.blk_count)])

    def over_rest(self, array, distance):
        pairs = [(i, i ^ (2 * distance)) for i in range(2 * self.rest_count)]
        return lax.ppermute(array, "batch", pairs)

    def reduce_blk(self, mine, send):
        got = self.swap_cores(send)
        size = mine.shape[0] // self.blk_count
        parts = []
        for distance in range(self.blk_count):
            rows = slice(distance * size, (distance + 1) * size)
            parts.append(added([mine[rows], got[rows]]))
        return [parts[0]] + [self.over_blk(parts[d], d) for d in range(1, self.blk_count)]

    def reduce_rest(self, arrays):
        size = arrays[0].shape[0] // self.rest_count
        shares = []
        for distance in range(self.rest_count):
            start = (self.rest ^ distance) * size
            shares.append(added([lax.dynamic_slice_in_dim(a, start, size, 0) for a in arrays]))
        got = [self.over_rest(shares[d], d) for d in range(1, self.rest_count)]
        share = added([shares[0]] + got)
        return [share] + [self.over_rest(share, d) for d in range(1, self.rest_count)]

    def reduce_rest_small(self, arrays):
        piece = added(arrays)
        return added([piece] + [self.over_rest(piece, d) for d in range(1, self.rest_count)])

    def gather_blk(self, piece):
        own = [piece] + [self.over_blk(piece, d) for d in range(1, self.blk_count)]
        return own, [self.swap_cores(part) for part in own]


def on_device(
    blk_count,
    batch_count,
    hidden_in,
    lengths,
    attn_gain,
    w_query,
    w_key,
    w_value,
    w_output,
    mlp_gain,
    w_gate,
    w_up,
    w_down,
    cotangent,
):
    seqs, positions, width = hidden_in.shape
    ff = w_gate.shape[1]
    count = blk_count
    devices = blk_count * batch_count
    slots = -(-seqs // count)
    wide = GROUPS * positions
    blk = lax.axis_index("blk")
    x_t = jnp.swapaxes(hidden_in, 1, 2)
    cot_t = jnp.swapaxes(cotangent, 1, 2)

    numbers = jnp.arange(seqs, dtype=jnp.int32)
    ahead = (lengths[None, :] > lengths[:, None]) | (
        (lengths[None, :] == lengths[:, None]) & (numbers[None, :] < numbers[:, None])
    )
    rank = jnp.sum(ahead.astype(jnp.int32), 1)
    slot_of, place = rank // count, rank % count
    owner = jnp.where(slot_of % 2 == 0, place, count - 1 - place)
    wanted_device = blk ^ jnp.repeat(jnp.arange(count, dtype=jnp.int32), slots)
    wanted_slot = jnp.tile(jnp.arange(slots, dtype=jnp.int32), count)
    match = (
        (owner[None, :] == wanted_device[:, None]) & (slot_of[None, :] == wanted_slot[:, None])
    ).astype(jnp.int32)
    sequence = jnp.sum(match * numbers[None, :], 1)
    own_lengths = jnp.sum(match[:slots] * lengths[None, :], 1)
    batch = lax.axis_index("batch")
    info = jnp.concatenate(
        [own_lengths, jnp.stack([blk]), sequence, jnp.stack([batch % 2, batch // 2])]
        + [owner ^ blk, slot_of]
    ).astype(jnp.int32)
    bit_at = first_bit(count, slots)
    total = Sum(blk_count, batch_count)

    frequency = np.float32(THETA) ** (
        -np.arange(HALF, dtype=np.float32) * np.float32(2.0) / np.float32(HEAD_DIM)
    )
    places = np.arange(count * positions, dtype=np.float32).reshape(count, 1, positions)
    angles = (frequency[None, :, None] * places).astype(np.float32)
    cos_table, sin_table = jnp.asarray(np.cos(angles)), jnp.asarray(np.sin(angles))
    gain_first = attn_gain.astype(F32)[:, None]
    gain_second = mlp_gain.astype(F32)[:, None]
    moved = jax.ShapeDtypeStruct((slots, width, positions), BF16)

    def spread(array, name):
        def source(distance):
            return pl.BlockSpec(
                (1, width, positions),
                lambda slot, info: (info[slots + 1 + distance * slots + slot], 0, 0),
            )

        picked = call(
            functools.partial(pick, count),
            name,
            (slots,),
            [source(distance) for distance in range(count)],
            [per_step(width, positions)] * count,
            [moved] * count,
        )(info, *[array] * count)
        got = [picked[0]]
        for distance in range(1, count):
            pairs = [(i, i ^ distance) for i in range(count)]
            got.append(lax.ppermute(picked[distance], "blk", pairs))
        return got

    def collect(parts, name):
        got = [parts[0]]
        for distance in range(1, count):
            pairs = [(i, i ^ distance) for i in range(count)]
            got.append(lax.ppermute(parts[distance], "blk", pairs))
        last = bit_at + 2

        def source(which):
            def where(seq, info):
                mine = info[last + seq] == which
                return (jnp.where(mine, info[last + seqs + seq], 0), 0, 0)

            return pl.BlockSpec((1, width, positions), where)

        return call(
            functools.partial(put, count, last),
            name,
            (seqs,),
            [source(distance) for distance in range(count)],
            per_step(width, positions),
            jax.ShapeDtypeStruct((seqs, width, positions), BF16),
        )(info, *got)

    x_moved = spread(x_t, "pick_hidden")
    cot_moved = spread(cot_t, "pick_cotangent")

    table = whole(count, HALF, positions)
    blocks_of = lambda rows: per_step(count, rows, positions)
    unit_flops = 4 * slots * count * positions * positions * HEADS * 256
    dense = 2 * slots * count * positions * width
    normed, queries, kv, mix, log_total = call(
        functools.partial(front, positions, count),
        "front",
        (slots,),
        [per_step(width, positions)] * count
        + [whole(width, 1), whole(Q_WIDTH, width), whole(2 * KV_WIDTH, width), table, table],
        [
            blocks_of(width),
            blocks_of(Q_WIDTH),
            blocks_of(2 * KV_WIDTH),
            blocks_of(Q_WIDTH),
            per_step(count, KV_HEADS, wide),
        ],
        [
            jax.ShapeDtypeStruct((slots, count, width, positions), BF16),
            jax.ShapeDtypeStruct((slots, count, Q_WIDTH, positions), BF16),
            jax.ShapeDtypeStruct((slots, count, 2 * KV_WIDTH, positions), BF16),
            jax.ShapeDtypeStruct((slots, count, Q_WIDTH, positions), BF16),
            jax.ShapeDtypeStruct((slots, count, KV_HEADS, wide), F32),
        ],
        [pltpu.VMEM((2 * KV_HEADS, wide), F32), pltpu.VMEM((KV_WIDTH, wide), F32)],
        flops=dense * 960 + 2 * unit_flops,
    )(
        info,
        *x_moved,
        gain_first,
        w_query.T,
        jnp.concatenate([w_key.T, w_value.T], 0),
        cos_table,
        sin_table,
    )

    first_shapes = [(width, ff), (width, ff), (width, ff), (Q_WIDTH, width)]
    first_rows = sum(packed_rows(*shape) for shape in first_shapes)
    unit = 16 * devices
    first_half = -(-first_rows // unit) * unit // 2

    def arrived(distance):
        def where(step, info):
            now = lax.div(step, slots)
            slot = jnp.where(now < distance, 0, slots - 1)
            return (jnp.where(now == distance, lax.rem(step, slots), slot), 0, 0)

        return pl.BlockSpec((1, width, positions), where)

    def block_spec(*shape):
        zeros = (0,) * len(shape)

        def where(step, info):
            return (lax.rem(step, slots), info[slots] ^ lax.div(step, slots)) + zeros

        return pl.BlockSpec((1, 1) + shape, where)

    arrivals = [arrived(distance) for distance in range(count)]
    *layer_t, grad_middle, grad_attn, deltas, mine_first, send_first, gain_sum = call(
        functools.partial(feed_forward, positions, 512, count, slots),
        "feed_forward",
        (slots * count,),
        arrivals * 2
        + [
            block_spec(Q_WIDTH, positions),
            whole(width, 1),
            whole(width, Q_WIDTH),
            whole(Q_WIDTH, width),
            whole(ff, width),
            whole(width, ff),
            whole(ff, width),
            whole(width, ff),
            whole(width, ff),
            whole(ff, width),
        ],
        arrivals
        + [
            block_spec(width, positions),
            block_spec(Q_WIDTH, positions),
            block_spec(KV_HEADS, wide),
            kept(first_half, LANES),
            kept(first_half, LANES),
            kept(width, positions),
        ],
        [moved] * count
        + [
            jax.ShapeDtypeStruct((slots, count, width, positions), BF16),
            jax.ShapeDtypeStruct((slots, count, Q_WIDTH, positions), BF16),
            jax.ShapeDtypeStruct((slots, count, KV_HEADS, wide), F32),
            jax.ShapeDtypeStruct((first_half, LANES), BF16),
            jax.ShapeDtypeStruct((first_half, LANES), BF16),
            jax.ShapeDtypeStruct((width, positions), F32),
        ],
        [pltpu.VMEM(shape, F32) for shape in first_shapes]
        + [pltpu.VMEM((width, positions), BF16)] * 3,
        flops=9 * dense * ff,
    )(
        info,
        *x_moved,
        *cot_moved,
        mix,
        gain_second,
        w_output.T,
        w_output,
        w_gate.T,
        w_gate,
        w_up.T,
        w_up,
        w_down.T,
        w_down,
    )

    parts_first = total.reduce_blk(mine_first, send_first)

    second_shapes = [(width, Q_WIDTH), (KV_WIDTH, width), (KV_WIDTH, width)]
    second_rows = sum(packed_rows(*shape) for shape in second_shapes)
    second_rows += -(-2 * len(pieces_of(width)) // 16) * 16
    second_half = -(-second_rows // unit) * unit // 2
    lin_width = Q_WIDTH + 2 * KV_WIDTH
    grad_lin = call(
        functools.partial(attend_back, positions, count),
        "attend_back",
        (slots,),
        [
            blocks_of(Q_WIDTH),
            blocks_of(2 * KV_WIDTH),
            blocks_of(Q_WIDTH),
            per_step(count, KV_HEADS, wide),
            per_step(count, KV_HEADS, wide),
            table,
            table,
        ],
        blocks_of(lin_width),
        jax.ShapeDtypeStruct((slots, count, lin_width, positions), BF16),
        [
            pltpu.VMEM((KV_WIDTH, wide), F32),
            pltpu.VMEM((count, 2 * KV_WIDTH, positions), F32),
        ],
        flops=5 * unit_flops,
        after=[parts_first[0]],
    )(info, queries, kv, grad_attn, log_total, deltas, cos_table, sin_table)

    *grad_in_t, mine_second, send_second = call(
        functools.partial(project_back, positions, count, slots),
        "project_back",
        (slots * count,),
        arrivals
        + [
            whole(width, 1),
            block_spec(width, positions),
            block_spec(lin_width, positions),
            block_spec(width, positions),
            whole(width, lin_width),
            whole(width, positions),
        ],
        arrivals + [kept(second_half, LANES), kept(second_half, LANES)],
        [moved] * count
        + [
            jax.ShapeDtypeStruct((second_half, LANES), BF16),
            jax.ShapeDtypeStruct((second_half, LANES), BF16),
        ],
        [
            pltpu.VMEM((width, positions), F32),
            pltpu.VMEM((width, Q_WIDTH), F32),
            pltpu.VMEM((KV_WIDTH, width), F32),
            pltpu.VMEM((KV_WIDTH, width), F32),
        ]
        + [pltpu.VMEM((width, positions), BF16)] * 2,
        flops=2 * dense * 960,
        after=parts_first[1:],
    )(
        info,
        *x_moved,
        gain_first,
        normed,
        grad_lin,
        grad_middle,
        jnp.concatenate([w_query, w_key, w_value], 1),
        gain_sum,
    )
    layer_out = collect(layer_t, "put_layer")
    grad_in = collect(grad_in_t, "put_grad")

    shares = total.reduce_rest(parts_first)
    share_rows = shares[0].shape[0]
    rest_count = batch_count // 2
    piece_first = call(
        functools.partial(line_up, rest_count, bit_at + 1),
        "line_up",
        (1,),
        [whole(share_rows, LANES)] * rest_count,
        whole(rest_count * share_rows, LANES),
        jax.ShapeDtypeStruct((rest_count * share_rows, LANES), BF16),
        after=[layer_out, grad_in],
    )(info, *shares)
    piece_second = total.reduce_rest_small(total.reduce_blk(mine_second, send_second))
    own, other = total.gather_blk(jnp.concatenate([piece_first, piece_second], 0))
    size_first, size_second = piece_first.shape[0], piece_second.shape[0]

    def open_up(shapes, gain_width, start, size, name):
        outs = list(shapes) + ([(1, gain_width)] * 2 if gain_width else [])
        return call(
            functools.partial(unpack, count, slots, shapes, gain_width, start, size),
            name,
            (1,),
            [whole(*own[0].shape)] * (2 * count),
            [whole(*shape) for shape in outs],
            [jax.ShapeDtypeStruct(shape, F32) for shape in outs],
            [pltpu.VMEM((2 * count * size, LANES), BF16)],
            bytes_accessed=12 * count * size * LANES,
        )(info, *own, *other)

    g_gate, g_up, g_down_t, g_out = open_up(first_shapes, 0, 0, size_first, "unpack_first")
    g_query, g_key_t, g_value_t, gain_one, gain_two = open_up(
        second_shapes, width, size_first, size_second, "unpack_second"
    )
    return (
        jnp.swapaxes(layer_out, 1, 2),
        jnp.swapaxes(grad_in, 1, 2),
        gain_one.reshape(width),
        g_query,
        g_key_t.T,
        g_value_t.T,
        g_out,
        gain_two.reshape(width),
        g_gate,
        g_up,
        g_down_t.T,
    )


def solution(mesh):
    rows = P("batch", "blk", None)
    return jax.shard_map(
        functools.partial(on_device, mesh.shape["blk"], mesh.shape["batch"]),
        mesh=mesh,
        in_specs=(rows, P("batch")) + (P(),) * 9 + (rows,),
        out_specs=(rows, rows) + (P(),) * 9,
        check_vma=False,
    )
```

```python
import functools

import jax
import jax.numpy as jnp
import numpy as np
from jax import lax
from jax.experimental import pallas as pl
from jax.experimental.pallas import tpu as pltpu
from jax.sharding import PartitionSpec as P

HEADS = 9
KV_HEADS = 3
HEAD_DIM = 64
GROUPS = HEADS // KV_HEADS
HALF = HEAD_DIM // 2
KV_WIDTH = KV_HEADS * HEAD_DIM
Q_WIDTH = HEADS * HEAD_DIM

EPS = 1e-05
THETA = 10000.0
NEGATIVE = -1e30
LANES = 128
F32 = jnp.float32
BF16 = jnp.bfloat16
VMEM_LIMIT = 60 * 1024 * 1024

NN = (((1,), (0,)), ((), ()))
NT = (((1,), (1,)), ((), ()))
TN = (((0,), (0,)), ((), ()))


def dot(a, b, dims=NN):
    return lax.dot_general(a, b, dims, preferred_element_type=F32)


def call(
    kernel, name, grid, in_specs, out_specs, out_shape, scratch=(), flops=0, bytes_accessed=0, after=()
):
    count, more = len(in_specs), len(after)

    def body(info, *refs):
        kernel(info, *refs[:count], *refs[count + more :])

    made = pl.pallas_call(
        body,
        grid_spec=pltpu.PrefetchScalarGridSpec(
            num_scalar_prefetch=1,
            grid=grid,
            in_specs=list(in_specs) + [pl.BlockSpec(memory_space=pl.ANY)] * more,
            out_specs=out_specs,
            scratch_shapes=list(scratch),
        ),
        out_shape=out_shape,
        compiler_params=pltpu.CompilerParams(
            dimension_semantics=("arbitrary",), vmem_limit_bytes=VMEM_LIMIT
        ),
        cost_estimate=pl.CostEstimate(
            flops=int(flops), bytes_accessed=int(bytes_accessed), transcendentals=0
        ),
        name=name,
    )
    return lambda *operands: made(*operands, *after)


def per_step(*shape):
    zeros = (0,) * len(shape)
    return pl.BlockSpec((1,) + shape, lambda s, info: (s,) + zeros)


def whole(*shape):
    zeros = (0,) * len(shape)
    return pl.BlockSpec(shape, lambda s, info: zeros, pipeline_mode=pl.Buffered(1))


def kept(*shape):
    zeros = (0,) * len(shape)
    return pl.BlockSpec(shape, lambda s, info: zeros)


def valid_rows(info, slot, block, positions):
    return jnp.clip(info[slot] - block * positions, 0, positions)


def first_bit(count, slots):
    return slots + 1 + count * slots


def pick(count, info, *refs):
    for distance in range(count):
        refs[count + distance][...] = refs[distance][...]


def put(count, slots, last, info, *refs):
    place = place_of(info[last + pl.program_id(0)], info[first_bit(count, slots)], count)
    for which in range(count):

        @pl.when(place == which)
        def _():
            refs[count][0] = refs[which][0, 0]


def rotate(lin, cos, sin, heads, store):
    for head in range(heads):
        low = head * HEAD_DIM
        lead, trail = lin[low : low + HALF], lin[low + HALF : low + HEAD_DIM]
        store(low, (lead * cos - trail * sin).astype(BF16))
        store(low + HALF, (trail * cos + lead * sin).astype(BF16))


def front(positions, count, info, *refs):
    x_refs, refs = refs[:count], refs[count:]
    gain_ref, wq_ref, wk_t_ref, wv_t_ref, cos_ref, sin_ref = refs[:6]
    normed_ref, q_ref, kv_ref, mix_ref, log_ref, stat, acc = refs[6:]
    slot = pl.program_id(0)
    blk = info[pl.num_programs(0)]
    blocks = lax.div(info[slot] + positions - 1, positions)

    for distance in range(count):
        block = blk ^ distance

        @pl.when(block < blocks)
        def _():
            x = x_refs[distance][0].astype(F32)
            scaled = lax.rsqrt(jnp.mean(x * x, axis=0, keepdims=True) + EPS)
            normed = (x * scaled * gain_ref[...]).astype(BF16)
            normed_ref[0, block] = normed
            cos, sin = cos_ref[block], sin_ref[block]

            def store_kv(low, value):
                kv_ref[0, block, low : low + HALF] = value

            rotate(dot(wk_t_ref[...], normed), cos, sin, KV_HEADS, store_kv)
            kv_ref[0, block, KV_WIDTH:] = dot(wv_t_ref[...], normed).astype(BF16)

            def store_q(low, value):
                q_ref[0, block, low : low + HALF] = value

            rotate(dot(wq_ref[...], normed) * (HEAD_DIM**-0.5), cos, sin, HEADS, store_q)

    def visit(block, other, diagonal):
        if diagonal:
            mask = causal_mask(positions, GROUPS)
        lows = [group * HEAD_DIM for group in range(KV_HEADS)]
        keys = [kv_ref[0, other, low : low + HEAD_DIM] for low in lows]
        values = [kv_ref[0, other, KV_WIDTH + low : KV_WIDTH + low + HEAD_DIM] for low in lows]
        asked = [heads_side_by_side(q_ref, block, group) for group in range(KV_HEADS)]
        if not diagonal:
            olds = [stat[group : group + 1] for group in range(KV_HEADS)]
            sums = [stat[KV_HEADS + group : KV_HEADS + group + 1] for group in range(KV_HEADS)]
            accs = [acc[low : low + HEAD_DIM] for low in lows]
        scores = [dot(keys[group], asked[group], TN) for group in range(KV_HEADS)]
        peaks, totals, mixes = [], [], []
        for group in range(KV_HEADS):
            score = scores[group]
            if diagonal:
                score = jnp.where(mask, score, NEGATIVE)
            peak = jnp.max(score, axis=0, keepdims=True)
            if not diagonal:
                peak = jnp.maximum(peak, olds[group])
            weights = jnp.exp(score - peak)
            total = jnp.sum(weights, axis=0, keepdims=True)
            summed = dot(values[group], weights.astype(BF16))
            if not diagonal:
                fade = jnp.exp(olds[group] - peak)
                total = total + sums[group] * fade
                summed = summed + accs[group] * fade
            peaks.append(peak)
            totals.append(total)
            mixes.append(summed)
        for group, low in enumerate(lows):
            stat[group : group + 1] = peaks[group]
            stat[KV_HEADS + group : KV_HEADS + group + 1] = totals[group]
            acc[low : low + HEAD_DIM] = mixes[group]

    def one_block(block, carry):
        visit(block, block, True)

        def one_pair(other, carry):
            visit(block, other, False)
            return carry

        lax.fori_loop(0, block, one_pair, 0)
        log_ref[0, block] = stat[:KV_HEADS] + jnp.log(stat[KV_HEADS:])
        for group in range(KV_HEADS):
            low = group * HEAD_DIM
            share = 1.0 / stat[KV_HEADS + group : KV_HEADS + group + 1]
            mix = (acc[low : low + HEAD_DIM] * share).astype(BF16)
            for place in range(GROUPS):
                row = (group * GROUPS + place) * HEAD_DIM
                mix_ref[0, block, row : row + HEAD_DIM] = mix[
                    :, place * positions : (place + 1) * positions
                ]
        return carry

    lax.fori_loop(0, blocks, one_block, 0)


def causal_mask(positions, copies):
    keys = lax.broadcasted_iota(jnp.int32, (positions, positions), 0)
    queries = lax.broadcasted_iota(jnp.int32, (positions, positions), 1)
    return jnp.concatenate([keys <= queries] * copies, 1)


def heads_side_by_side(ref, block, group):
    first = group * GROUPS * HEAD_DIM
    return jnp.concatenate(
        [ref[0, block, first + p * HEAD_DIM : first + (p + 1) * HEAD_DIM] for p in range(GROUPS)],
        1,
    )


def pieces_of(columns):
    return [(start, min(LANES, columns - start)) for start in range(0, columns, LANES)]


def place_of(distance, core, count):
    if count == 4:
        return distance ^ (3 * (((distance ^ (distance >> 1)) & 1) * core))
    return distance


class Parts:
    def __init__(self, halves, count, blk):
        self.halves, self.count, self.blk = halves, count, blk
        self.size = halves[0].shape[0] // count

    def write(self, row, value):
        done, rows = 0, value.shape[0]
        while done < rows:
            part, inside = divmod(row + done, self.size)
            take = min(self.size - inside, rows - done)
            half, part = divmod(part, self.count)
            place = place_of(part ^ self.blk, half, self.count)
            start = pl.multiple_of(place * self.size + inside, 16)
            self.halves[half][pl.ds(start, take)] = value[done : done + take]
            done += take


def pack_into(parts, row, acc):
    rows, columns = acc.shape
    for start, width in pieces_of(columns):
        part = acc[:, start : start + width].astype(BF16)
        if width < LANES:
            half = rows // 2
            part = jnp.concatenate([part[:half], part[half:]], 1)
        parts.write(row, part)
        row += part.shape[0]
    return row


def gain_rows(acc):
    ones = jnp.ones((16, acc.shape[1]), BF16)
    sums = dot(ones, acc[...].astype(BF16), NT)[:1]
    parts = [sums[:, start : start + width] for start, width in pieces_of(sums.shape[1])]
    short = LANES - parts[-1].shape[1]
    if short:
        parts[-1] = jnp.concatenate([parts[-1], jnp.zeros((1, short), F32)], 1)
    return parts


def pack_all(info, bit_at, count, blk, mine_ref, send_ref, accs, last=None):
    def fill(halves):
        parts = Parts(halves, count, blk)
        row = 0
        for acc in accs:
            row = pack_into(parts, row, acc)
        if last is not None:
            parts.write(row, last)
            row += last.shape[0]
        rest = 2 * mine_ref.shape[0] - row
        if rest:
            parts.write(row, jnp.zeros((rest, LANES), BF16))

    pl.when(info[bit_at] == 0)(lambda: fill((mine_ref, send_ref)))
    pl.when(info[bit_at] != 0)(lambda: fill((send_ref, mine_ref)))


def packed_rows(rows, columns):
    return rows * columns // LANES


def pick_block(refs, distance, out_ref, wanted):
    for which, ref in enumerate(refs):

        @pl.when(jnp.logical_and(wanted, distance == which))
        def _():
            out_ref[...] = ref[0]


def place_groups(count):
    return [[0, 1], [2, 3]] if count == 4 else [[place] for place in range(count)]


def place_block(refs, count, place, value_ref):
    for ref, group in zip(refs, place_groups(count)):
        inside = jnp.logical_and(place >= group[0], place <= group[-1])

        @pl.when(inside)
        def _():
            ref[0, 0] = value_ref[...]


def normalised(value):
    scaled = lax.rsqrt(jnp.mean(value * value, axis=0, keepdims=True) + EPS)
    return value * scaled, scaled


def norm_back(upstream, gain, normal, scaled):
    inner = upstream * gain
    return scaled * (inner - normal * jnp.mean(inner * normal, axis=0, keepdims=True))


def valid_lanes(rows, positions):
    lane = lax.broadcasted_iota(jnp.int32, (1, positions), 1)
    return (lane < rows).astype(F32)


def feed_forward(positions, chunk, count, slots, info, *refs):
    x_refs, cot_refs, refs = refs[:count], refs[count : 2 * count], refs[2 * count :]
    mix_ref, gain_ref, wo_t_ref, wo_ref, wg_t_ref, wg_ref, wu_t_ref, wu_ref, wd_t_ref, wd_ref = refs[
        :10
    ]
    groups = len(place_groups(count))
    out_refs, refs = refs[10 : 10 + groups], refs[10 + groups :]
    mid_ref, gattn_ref, delta_ref, mine_ref, send_ref, gain_sum_ref = refs[:6]
    acc_gate, acc_up, acc_down, acc_out, x_now, cot_now, out_now = refs[6:]
    step = pl.program_id(0)
    place, slot = lax.div(step, slots), lax.rem(step, slots)
    distance = place_of(place, info[first_bit(count, slots)], count)
    rows = valid_rows(info, slot, info[slots] ^ distance, positions)
    width = x_now.shape[0]
    hidden_width = wg_ref.shape[1]

    @pl.when(step == 0)
    def _():
        for acc in (acc_gate, acc_up, acc_down, acc_out, gain_sum_ref):
            acc[...] = jnp.zeros_like(acc)

    @pl.when(rows <= 0)
    def _():
        out_now[...] = jnp.zeros_like(out_now)

    pick_block(x_refs, distance, x_now, rows > 0)
    pick_block(cot_refs, distance, cot_now, rows > 0)

    @pl.when(rows > 0)
    def _():
        valid = valid_lanes(rows, positions)
        mix = mix_ref[0, 0]
        middle = x_now[...].astype(F32) + dot(wo_t_ref[...], mix)
        normal, scaled = normalised(middle)
        gain = gain_ref[...]
        normed = (normal * gain).astype(BF16)
        grad_y = cot_now[...].astype(F32) * valid
        grad_low = grad_y.astype(BF16)
        branch = jnp.zeros((width, positions), F32)
        grad_normed = jnp.zeros((width, positions), F32)
        for start in range(0, hidden_width, chunk):
            part = slice(start, start + chunk)
            gate = dot(wg_t_ref[part], normed)
            up = dot(wu_t_ref[part], normed)
            grad_hidden = dot(wd_ref[part], grad_low)
            sig = 1.0 / (1.0 + jnp.exp(-gate))
            act = gate * sig
            hidden = (act * up).astype(BF16)
            grad_gate = (grad_hidden * up * (sig * (1.0 + gate * (1.0 - sig)))).astype(BF16)
            grad_up = (grad_hidden * act).astype(BF16)
            branch = branch + dot(wd_t_ref[:, part], hidden)
            grad_normed = grad_normed + dot(wg_ref[:, part], grad_gate)
            grad_normed = grad_normed + dot(wu_ref[:, part], grad_up)
            acc_down[:, part] += dot(grad_low, hidden, NT)
            acc_gate[:, part] += dot(normed, grad_gate, NT)
            acc_up[:, part] += dot(normed, grad_up, NT)
        out_now[...] = (valid * (middle + branch)).astype(BF16)
        gain_sum_ref[...] += grad_normed * normal
        grad_middle = grad_y + norm_back(grad_normed, gain, normal, scaled)
        grad_mid_low = grad_middle.astype(BF16)
        mid_ref[0, 0] = grad_mid_low
        acc_out[...] += dot(mix, grad_mid_low, NT)
        grad_attn = dot(wo_ref[...], grad_mid_low).astype(BF16)
        gattn_ref[0, 0] = grad_attn
        product = grad_attn.astype(F32) * mix.astype(F32)
        for head in range(HEADS):
            part = slice(head * HEAD_DIM, (head + 1) * HEAD_DIM)
            group, turn = head // GROUPS, head % GROUPS
            lanes = slice(turn * positions, (turn + 1) * positions)
            delta_ref[0, 0, group : group + 1, lanes] = jnp.sum(
                product[part], axis=0, keepdims=True
            )

    place_block(out_refs, count, place, out_now)

    @pl.when(step == count * slots - 1)
    def _():
        pack_all(
            info,
            first_bit(count, slots),
            count,
            info[slots],
            mine_ref,
            send_ref,
            (acc_gate, acc_up, acc_down, acc_out),
        )


def rotate_back(value, cos, sin, heads):
    parts = []
    for head in range(heads):
        low = head * HEAD_DIM
        lead, trail = value[low : low + HALF], value[low + HALF : low + HEAD_DIM]
        parts += [lead * cos + trail * sin, trail * cos - lead * sin]
    return jnp.concatenate(parts, 0)


def attend_back(positions, count, info, *refs):
    q_ref, kv_ref, gattn_ref, log_ref, delta_ref, cos_ref, sin_ref = refs[:7]
    lin_ref, dq, dkv = refs[7:]
    blocks = lax.div(info[pl.program_id(0)] + positions - 1, positions)

    def visit(block, other, diagonal):
        if diagonal:
            mask = causal_mask(positions, GROUPS)
        lows = [group * HEAD_DIM for group in range(KV_HEADS)]
        keys = [kv_ref[0, other, low : low + HEAD_DIM] for low in lows]
        values = [kv_ref[0, other, KV_WIDTH + low : KV_WIDTH + low + HEAD_DIM] for low in lows]
        asked = [heads_side_by_side(q_ref, block, group) for group in range(KV_HEADS)]
        grads = [heads_side_by_side(gattn_ref, block, group) for group in range(KV_HEADS)]
        logs = [log_ref[0, block, group : group + 1] for group in range(KV_HEADS)]
        deltas = [delta_ref[0, block, group : group + 1] for group in range(KV_HEADS)]
        results = []
        for group in range(KV_HEADS):
            scores = dot(keys[group], asked[group], TN)
            grad_probs = dot(values[group], grads[group], TN)
            probs = jnp.exp(scores - logs[group])
            if diagonal:
                probs = jnp.where(mask, probs, 0.0)
            grad_scores = (probs * (grad_probs - deltas[group])).astype(BF16)
            grad_value = dot(grads[group], probs.astype(BF16), NT)
            grad_query = dot(keys[group], grad_scores)
            grad_key = dot(asked[group], grad_scores, NT)
            results.append((grad_query, grad_key, grad_value))
        for low, (grad_query, grad_key, grad_value) in zip(lows, results):
            rows = slice(low, low + HEAD_DIM)
            more = slice(KV_WIDTH + low, KV_WIDTH + low + HEAD_DIM)
            if diagonal:
                dq[rows] = grad_query
                dkv[other, rows] = grad_key
                dkv[other, more] = grad_value
            else:
                dq[rows] += grad_query
                dkv[other, rows] += grad_key
                dkv[other, more] += grad_value

    def one_block(block, carry):
        visit(block, block, True)

        def one_pair(other, carry):
            visit(block, other, False)
            return carry

        lax.fori_loop(0, block, one_pair, 0)
        grad = jnp.concatenate(
            [
                dq[
                    (head // GROUPS) * HEAD_DIM : (head // GROUPS + 1) * HEAD_DIM,
                    (head % GROUPS) * positions : (head % GROUPS + 1) * positions,
                ]
                for head in range(HEADS)
            ],
            0,
        ) * (HEAD_DIM**-0.5)
        lin = rotate_back(grad, cos_ref[block], sin_ref[block], HEADS)
        lin_ref[0, block, :Q_WIDTH] = lin.astype(BF16)
        return carry

    lax.fori_loop(0, blocks, one_block, 0)

    def one_rotation(block, carry):
        grad = dkv[block]
        rotated = rotate_back(grad[:KV_WIDTH], cos_ref[block], sin_ref[block], KV_HEADS)
        lin_ref[0, block, Q_WIDTH : Q_WIDTH + KV_WIDTH] = rotated.astype(BF16)
        lin_ref[0, block, Q_WIDTH + KV_WIDTH :] = grad[KV_WIDTH:].astype(BF16)
        return carry

    lax.fori_loop(0, blocks, one_rotation, 0)


def project_back(positions, count, slots, info, *refs):
    x_refs, refs = refs[:count], refs[count:]
    gain_ref, normed_ref, lin_ref, mid_ref, wq_ref, wk_t_ref, wv_t_ref, other_gain_ref = refs[:8]
    groups = len(place_groups(count))
    out_refs, refs = refs[8 : 8 + groups], refs[8 + groups :]
    mine_ref, send_ref, gain_sum, acc_q, acc_k, acc_v, x_now, out_now = refs
    step = pl.program_id(0)
    place, slot = lax.div(step, slots), lax.rem(step, slots)
    distance = place_of(place, info[first_bit(count, slots)], count)
    blk = info[slots]
    rows = valid_rows(info, slot, blk ^ distance, positions)

    @pl.when(step == 0)
    def _():
        for acc in (acc_q, acc_k, acc_v, gain_sum):
            acc[...] = jnp.zeros_like(acc)

    pick_block(x_refs, distance, x_now, rows > 0)

    @pl.when(rows <= 0)
    def _():
        out_now[...] = jnp.zeros_like(out_now)

    @pl.when(rows > 0)
    def _():
        lin = lin_ref[0, 0]
        normed = normed_ref[0, 0]
        acc_q[...] += dot(normed, lin[:Q_WIDTH], NT)
        acc_k[...] += dot(lin[Q_WIDTH : Q_WIDTH + KV_WIDTH], normed, NT)
        acc_v[...] += dot(lin[Q_WIDTH + KV_WIDTH :], normed, NT)
        grad_normed = dot(wq_ref[...], lin[:Q_WIDTH])
        grad_normed += dot(wk_t_ref[...], lin[Q_WIDTH : Q_WIDTH + KV_WIDTH], TN)
        grad_normed += dot(wv_t_ref[...], lin[Q_WIDTH + KV_WIDTH :], TN)
        normal, scaled = normalised(x_now[...].astype(F32))
        gain_sum[...] += grad_normed * normal
        back = norm_back(grad_normed, gain_ref[...], normal, scaled)
        out_now[...] = (mid_ref[0, 0].astype(F32) + back).astype(BF16)

    place_block(out_refs, count, place, out_now)

    @pl.when(step == count * slots - 1)
    def _():
        gains = gain_rows(gain_sum) + gain_rows(other_gain_ref)
        gains.append(jnp.zeros((-len(gains) % 16, LANES), F32))
        gains = jnp.concatenate(gains, 0).astype(BF16)
        pack_all(
            info,
            first_bit(count, slots),
            count,
            blk,
            mine_ref,
            send_ref,
            (acc_q, acc_k, acc_v),
            gains,
        )


def unpack(count, slots, shapes, gain_width, info, *refs):
    out_refs, buffer = refs[2 * count : -1], refs[-1]
    size = refs[0].shape[0]
    core = info[first_bit(count, slots)]
    for which in range(2):
        for place in range(count):
            distance = place_of(place, core ^ which, count)
            part = (core ^ which) * count + (info[slots] ^ distance)
            buffer[pl.ds(pl.multiple_of(part * size, 16), size)] = refs[which * count + place][...]
    row = 0
    for ref, (rows, columns) in zip(out_refs, shapes):
        for first, width in pieces_of(columns):
            if width == LANES:
                ref[:, first : first + LANES] = buffer[row : row + rows].astype(F32)
                row += rows
            else:
                half = rows // 2
                part = buffer[row : row + half].astype(F32)
                ref[:half, first : first + width] = part[:, :width]
                ref[half:, first : first + width] = part[:, width:]
                row += half
    if gain_width:
        gains = buffer[row : row + 16].astype(F32)
        line = 0
        for ref in out_refs[len(shapes) :]:
            for first, width in pieces_of(gain_width):
                ref[:, first : first + width] = gains[line : line + 1, :width]
                line += 1


def line_up(bits, at, info, *refs):
    size = refs[0].shape[0]
    held = [0]
    for number, ref in enumerate(refs[:-1]):
        came = held if number == 0 else [place ^ bits[number - 1] for place in held]
        for line, place in enumerate(came):
            start = pl.multiple_of((info[at] ^ place) * size, 16)
            refs[-1][pl.ds(start, size)] = ref[line * size : (line + 1) * size]
        if number:
            held = held + came


def added(arrays):
    total = arrays[0].astype(F32)
    for array in arrays[1:]:
        total = total + array.astype(F32)
    return total.astype(BF16)


def bits_of(count):
    return count.bit_length() - 1


def later(value, *others):
    return lax.optimization_barrier((value, others))[0]


class Sum:
    def __init__(self, blk_count, batch_count):
        self.blk_count, self.rest_count = blk_count, batch_count // 2
        self.rest = lax.axis_index("batch") // 2
        self.bits = bits_of(self.rest_count)

    def swap_cores(self, array):
        pairs = [(i, i ^ 1) for i in range(2 * self.rest_count)]
        return lax.ppermute(array, "batch", pairs)

    def over_blk(self, array, distance):
        return lax.ppermute(array, "blk", [(i, i ^ distance) for i in range(self.blk_count)])

    def over_rest(self, array, bit):
        pairs = [(i, i ^ (2 << bit)) for i in range(2 * self.rest_count)]
        return lax.ppermute(array, "batch", pairs)

    def along(self, array, even, odd):
        pairs = []
        for blk in range(self.blk_count):
            for batch in range(2 * self.rest_count):
                to_blk = blk ^ (odd if batch % 2 else even)
                pairs.append(
                    (blk * 2 * self.rest_count + batch, to_blk * 2 * self.rest_count + batch)
                )
        return lax.ppermute(array, ("blk", "batch"), pairs)

    def reversed_rest(self):
        bits = [((self.rest >> k) & 1) << (self.bits - 1 - k) for k in range(self.bits)]
        return functools.reduce(lambda a, b: a | b, bits, jnp.int32(0))

    def parts_of_chip(self, mine, send):
        got = self.swap_cores(send)
        pieces = 2 if self.blk_count == 4 else self.blk_count
        size = mine.shape[0] // pieces
        return [
            added([array[n * size : (n + 1) * size] for array in (mine, got)])
            for n in range(pieces)
        ]

    def first_hop(self, parts):
        if self.blk_count == 4:
            return [parts[0], self.along(parts[1], 2, 1)]
        return [parts[0]] + [self.over_blk(parts[d], d) for d in range(1, self.blk_count)]

    def second_hop(self, arrays):
        if self.blk_count == 4:
            size = arrays[0].shape[0] // 2
            own = added([array[:size] for array in arrays])
            return [own, self.along(added([array[size:] for array in arrays]), 1, 2)]
        return arrays

    def send_half(self, arrays, k):
        half = arrays[0].shape[0] // 2
        side = (self.rest >> k) & 1

        def cut(which):
            return added([lax.dynamic_slice_in_dim(a, which * half, half, 0) for a in arrays])

        return [cut(side), self.over_rest(cut(1 - side), k)]

    def reduce_rest(self, arrays):
        for k in range(self.bits):
            arrays = self.send_half(arrays, k)
        return added(arrays)

    def gather_rest(self, share, before):
        got = [share]
        for k in reversed(range(self.bits)):
            if len(got) == 2:
                got = later(got, before)
            block = got[0] if len(got) == 1 else jnp.concatenate(got, 0)
            got.append(self.over_rest(block, k))
        return got

    def reduce_rest_small(self, piece):
        for k in range(self.bits):
            piece = added([piece, self.over_rest(piece, k)])
        return piece

    def gather_blk(self, piece, small):
        if self.blk_count == 4:
            one, two = self.along(piece, 1, 2), self.along(piece, 2, 1)
            own = [piece, one, two, self.along(one, 2, 1)]
        else:
            own = [piece] + [self.over_blk(piece, d) for d in range(1, self.blk_count)]
        if small:
            other = self.swap_cores(jnp.concatenate(own, 0))
            size = piece.shape[0]
            return own, [other[d * size : (d + 1) * size] for d in range(self.blk_count)]
        return own, [self.swap_cores(part) for part in own]


def on_device(
    blk_count,
    batch_count,
    hidden_in,
    lengths,
    attn_gain,
    w_query,
    w_key,
    w_value,
    w_output,
    mlp_gain,
    w_gate,
    w_up,
    w_down,
    cotangent,
):
    seqs, positions, width = hidden_in.shape
    ff = w_gate.shape[1]
    count = blk_count
    devices = blk_count * batch_count
    slots = -(-seqs // count)
    wide = GROUPS * positions
    blk = lax.axis_index("blk")
    x_t = jnp.swapaxes(hidden_in, 1, 2)
    cot_t = jnp.swapaxes(cotangent, 1, 2)

    numbers = jnp.arange(seqs, dtype=jnp.int32)
    ahead = (lengths[None, :] > lengths[:, None]) | (
        (lengths[None, :] == lengths[:, None]) & (numbers[None, :] < numbers[:, None])
    )
    rank = jnp.sum(ahead.astype(jnp.int32), 1)
    slot_of, place = rank // count, rank % count
    owner = jnp.where(slot_of % 2 == 0, place, count - 1 - place)
    wanted_device = blk ^ jnp.repeat(jnp.arange(count, dtype=jnp.int32), slots)
    wanted_slot = jnp.tile(jnp.arange(slots, dtype=jnp.int32), count)
    match = (
        (owner[None, :] == wanted_device[:, None]) & (slot_of[None, :] == wanted_slot[:, None])
    ).astype(jnp.int32)
    sequence = jnp.sum(match * numbers[None, :], 1)
    own_lengths = jnp.sum(match[:slots] * lengths[None, :], 1)
    batch = lax.axis_index("batch")
    total = Sum(blk_count, batch_count)
    info = jnp.concatenate(
        [own_lengths, jnp.stack([blk]), sequence, jnp.stack([batch % 2, total.reversed_rest()])]
        + [owner ^ blk, slot_of]
    ).astype(jnp.int32)
    bit_at = first_bit(count, slots)

    frequency = np.float32(THETA) ** (
        -np.arange(HALF, dtype=np.float32) * np.float32(2.0) / np.float32(HEAD_DIM)
    )
    places = np.arange(count * positions, dtype=np.float32).reshape(count, 1, positions)
    angles = (frequency[None, :, None] * places).astype(np.float32)
    cos_table, sin_table = jnp.asarray(np.cos(angles)), jnp.asarray(np.sin(angles))
    gain_first = attn_gain.astype(F32)[:, None]
    gain_second = mlp_gain.astype(F32)[:, None]
    moved = jax.ShapeDtypeStruct((slots, width, positions), BF16)

    def spread(array, name):
        def source(distance):
            return pl.BlockSpec(
                (1, width, positions),
                lambda slot, info: (info[slots + 1 + distance * slots + slot], 0, 0),
            )

        picked = call(
            functools.partial(pick, count),
            name,
            (slots,),
            [source(distance) for distance in range(count)],
            [per_step(width, positions)] * count,
            [moved] * count,
        )(info, *[array] * count)
        got = [picked[0]]
        for distance in range(1, count):
            pairs = [(i, i ^ distance) for i in range(count)]
            got.append(lax.ppermute(picked[distance], "blk", pairs))
        return got

    def place_at(info, place):
        return place_of(place, info[bit_at], count)

    def first_back(parts):
        if count == 4:
            return [(parts[0], 0), (parts[0], 1)], total.along(parts[1], 2, 1)
        got = [(parts[0], 0)]
        for distance in range(1, count):
            got.append((total.over_blk(parts[distance], distance), 0))
        return got, None

    def second_back(got, came):
        if count == 4:
            sent = jnp.concatenate([got[1][0][1:], came[1:]], 0)
            final = total.along(sent, 1, 2)
            return [got[0], (final, 0), (came, 0), (final, 1)]
        return got

    def collect(got, name):
        last = bit_at + 2

        def source(place, row):
            def where(seq, info):
                mine = place_at(info, info[last + seq]) == place
                return (row, jnp.where(mine, info[last + seqs + seq], 0), 0, 0)

            return pl.BlockSpec((1, 1, width, positions), where)

        return call(
            functools.partial(put, count, slots, last),
            name,
            (seqs,),
            [source(place, row) for place, (_, row) in enumerate(got)],
            per_step(width, positions),
            jax.ShapeDtypeStruct((seqs, width, positions), BF16),
        )(info, *[array for array, _ in got])

    x_moved = spread(x_t, "pick_hidden")
    cot_moved = spread(cot_t, "pick_cotangent")

    table = whole(count, HALF, positions)
    blocks_of = lambda rows: per_step(count, rows, positions)
    unit_flops = 4 * slots * count * positions * positions * HEADS * 256
    dense = 2 * slots * count * positions * width
    normed, queries, kv, mix, log_total = call(
        functools.partial(front, positions, count),
        "front",
        (slots,),
        [per_step(width, positions)] * count
        + [whole(width, 1), whole(Q_WIDTH, width)]
        + [whole(KV_WIDTH, width)] * 2
        + [table, table],
        [
            blocks_of(width),
            blocks_of(Q_WIDTH),
            blocks_of(2 * KV_WIDTH),
            blocks_of(Q_WIDTH),
            per_step(count, KV_HEADS, wide),
        ],
        [
            jax.ShapeDtypeStruct((slots, count, width, positions), BF16),
            jax.ShapeDtypeStruct((slots, count, Q_WIDTH, positions), BF16),
            jax.ShapeDtypeStruct((slots, count, 2 * KV_WIDTH, positions), BF16),
            jax.ShapeDtypeStruct((slots, count, Q_WIDTH, positions), BF16),
            jax.ShapeDtypeStruct((slots, count, KV_HEADS, wide), F32),
        ],
        [pltpu.VMEM((2 * KV_HEADS, wide), F32), pltpu.VMEM((KV_WIDTH, wide), F32)],
        flops=dense * 960 + 2 * unit_flops,
    )(
        info,
        *x_moved,
        gain_first,
        w_query.T,
        w_key.T,
        w_value.T,
        cos_table,
        sin_table,
    )

    first_shapes = [(width, ff), (width, ff), (width, ff), (Q_WIDTH, width)]
    first_rows = sum(packed_rows(*shape) for shape in first_shapes)
    unit = 16 * devices
    first_half = -(-first_rows // unit) * unit // 2

    def staying(now, slot, first, last):
        return jnp.where(now < first, 0, jnp.where(now > last, slots - 1, slot))

    def arrived(distance):
        def where(step, info):
            mine = place_at(info, distance)
            return (staying(lax.div(step, slots), lax.rem(step, slots), mine, mine), 0, 0)

        return pl.BlockSpec((1, width, positions), where)

    def leaving(group):
        def where(step, info):
            now = lax.div(step, slots)
            row = jnp.clip(now - group[0], 0, len(group) - 1)
            return (row, staying(now, lax.rem(step, slots), group[0], group[-1]), 0, 0)

        return pl.BlockSpec((1, 1, width, positions), where)

    def block_spec(*shape):
        zeros = (0,) * len(shape)

        def where(step, info):
            place = lax.div(step, slots)
            return (lax.rem(step, slots), info[slots] ^ place_at(info, place)) + zeros

        return pl.BlockSpec((1, 1) + shape, where)

    leavings = [leaving(group) for group in place_groups(count)]
    left = [
        jax.ShapeDtypeStruct((len(group), slots, width, positions), BF16)
        for group in place_groups(count)
    ]
    arrivals = [arrived(distance) for distance in range(count)]
    *layer_t, grad_middle, grad_attn, deltas, mine_first, send_first, gain_sum = call(
        functools.partial(feed_forward, positions, 512, count, slots),
        "feed_forward",
        (slots * count,),
        arrivals * 2
        + [
            block_spec(Q_WIDTH, positions),
            whole(width, 1),
            whole(width, Q_WIDTH),
            whole(Q_WIDTH, width),
            whole(ff, width),
            whole(width, ff),
            whole(ff, width),
            whole(width, ff),
            whole(width, ff),
            whole(ff, width),
        ],
        leavings
        + [
            block_spec(width, positions),
            block_spec(Q_WIDTH, positions),
            block_spec(KV_HEADS, wide),
            kept(first_half, LANES),
            kept(first_half, LANES),
            kept(width, positions),
        ],
        left
        + [
            jax.ShapeDtypeStruct((slots, count, width, positions), BF16),
            jax.ShapeDtypeStruct((slots, count, Q_WIDTH, positions), BF16),
            jax.ShapeDtypeStruct((slots, count, KV_HEADS, wide), F32),
            jax.ShapeDtypeStruct((first_half, LANES), BF16),
            jax.ShapeDtypeStruct((first_half, LANES), BF16),
            jax.ShapeDtypeStruct((width, positions), F32),
        ],
        [pltpu.VMEM(shape, F32) for shape in first_shapes]
        + [pltpu.VMEM((width, positions), BF16)] * 3,
        flops=9 * dense * ff,
    )(
        info,
        *x_moved,
        *cot_moved,
        mix,
        gain_second,
        w_output.T,
        w_output,
        w_gate.T,
        w_gate,
        w_up.T,
        w_up,
        w_down.T,
        w_down,
    )

    parts_first = total.parts_of_chip(mine_first, send_first)

    second_shapes = [(width, Q_WIDTH), (KV_WIDTH, width), (KV_WIDTH, width)]
    second_rows = sum(packed_rows(*shape) for shape in second_shapes)
    second_rows += -(-2 * len(pieces_of(width)) // 16) * 16
    second_half = -(-second_rows // unit) * unit // 2
    lin_width = Q_WIDTH + 2 * KV_WIDTH
    grad_lin = call(
        functools.partial(attend_back, positions, count),
        "attend_back",
        (slots,),
        [
            blocks_of(Q_WIDTH),
            blocks_of(2 * KV_WIDTH),
            blocks_of(Q_WIDTH),
            per_step(count, KV_HEADS, wide),
            per_step(count, KV_HEADS, wide),
            table,
            table,
        ],
        blocks_of(lin_width),
        jax.ShapeDtypeStruct((slots, count, lin_width, positions), BF16),
        [
            pltpu.VMEM((KV_WIDTH, wide), F32),
            pltpu.VMEM((count, 2 * KV_WIDTH, positions), F32),
        ],
        flops=5 * unit_flops,
        after=[parts_first[0]],
    )(info, queries, kv, grad_attn, log_total, deltas, cos_table, sin_table)

    layer_got, layer_came = first_back(layer_t)
    hop_first = total.first_hop(parts_first)
    hop_first, layer_came = later((hop_first, layer_came), grad_lin)
    hop_first = total.second_hop(hop_first)
    layer_got = second_back(layer_got, layer_came)

    *grad_in_t, mine_second, send_second = call(
        functools.partial(project_back, positions, count, slots),
        "project_back",
        (slots * count,),
        arrivals
        + [
            whole(width, 1),
            block_spec(width, positions),
            block_spec(lin_width, positions),
            block_spec(width, positions),
            whole(width, Q_WIDTH),
            whole(KV_WIDTH, width),
            whole(KV_WIDTH, width),
            whole(width, positions),
        ],
        leavings + [kept(second_half, LANES), kept(second_half, LANES)],
        left
        + [
            jax.ShapeDtypeStruct((second_half, LANES), BF16),
            jax.ShapeDtypeStruct((second_half, LANES), BF16),
        ],
        [
            pltpu.VMEM((width, positions), F32),
            pltpu.VMEM((width, Q_WIDTH), F32),
            pltpu.VMEM((KV_WIDTH, width), F32),
            pltpu.VMEM((KV_WIDTH, width), F32),
        ]
        + [pltpu.VMEM((width, positions), BF16)] * 2,
        flops=2 * dense * 960,
        after=[hop_first[0]],
    )(
        info,
        *x_moved,
        gain_first,
        normed,
        grad_lin,
        grad_middle,
        w_query,
        w_key.T,
        w_value.T,
        gain_sum,
    )
    hop_first = later(hop_first, mine_second)
    half_first = total.send_half(hop_first, 0)
    send_second, grad_in_t = later((send_second, grad_in_t), half_first[0])
    grad_got, grad_came = first_back(grad_in_t)
    half_first, arrays = later((half_first, [array for array, _ in layer_got]), mine_second)
    layer_got = [(array, row) for array, (_, row) in zip(arrays, layer_got)]
    for k in range(1, total.bits):
        half_first = total.send_half(half_first, k)
    layer_out = collect(layer_got, "put_layer")
    grad_got = second_back(grad_got, later(grad_came, half_first[0]))
    grad_in = collect(grad_got, "put_grad")
    parts_second = total.parts_of_chip(mine_second, send_second)
    piece_second = added(total.second_hop(total.first_hop(parts_second)))
    share = added(later(half_first, layer_out))
    held = total.gather_rest(share, grad_in)
    share_rows = share.shape[0]
    rest_count = batch_count // 2
    piece_first = call(
        functools.partial(line_up, [1 << k for k in range(total.bits)], bit_at + 1),
        "line_up",
        (1,),
        [whole(*array.shape) for array in held],
        whole(rest_count * share_rows, LANES),
        jax.ShapeDtypeStruct((rest_count * share_rows, LANES), BF16),
    )(info, *held)
    piece_second = total.reduce_rest_small(piece_second)

    def open_up(piece, small, shapes, gain_width, name):
        own, other = total.gather_blk(piece, small)
        size = piece.shape[0]
        outs = list(shapes) + ([(1, gain_width)] * 2 if gain_width else [])
        return call(
            functools.partial(unpack, count, slots, shapes, gain_width),
            name,
            (1,),
            [whole(size, LANES)] * (2 * count),
            [whole(*shape) for shape in outs],
            [jax.ShapeDtypeStruct(shape, F32) for shape in outs],
            [pltpu.VMEM((2 * count * size, LANES), BF16)],
            bytes_accessed=12 * count * size * LANES,
        )(info, *own, *other)

    g_gate, g_up, g_down_t, g_out = open_up(piece_first, False, first_shapes, 0, "unpack_first")
    g_query, g_key_t, g_value_t, gain_one, gain_two = open_up(
        piece_second, True, second_shapes, width, "unpack_second"
    )
    return (
        jnp.swapaxes(layer_out, 1, 2),
        jnp.swapaxes(grad_in, 1, 2),
        gain_one.reshape(width),
        g_query,
        g_key_t.T,
        g_value_t.T,
        g_out,
        gain_two.reshape(width),
        g_gate,
        g_up,
        g_down_t.T,
    )


def solution(mesh):
    rows = P("batch", "blk", None)
    return jax.shard_map(
        functools.partial(on_device, mesh.shape["blk"], mesh.shape["batch"]),
        mesh=mesh,
        in_specs=(rows, P("batch")) + (P(),) * 9 + (rows,),
        out_specs=(rows, rows) + (P(),) * 9,
        check_vma=False,
    )
```

```python
import functools

import jax
import jax.numpy as jnp
import numpy as np
from jax import lax
from jax.experimental import pallas as pl
from jax.experimental.pallas import tpu as pltpu
from jax.sharding import PartitionSpec as P

HEADS = 9
KV_HEADS = 3
HEAD_DIM = 64
GROUPS = HEADS // KV_HEADS
HALF = HEAD_DIM // 2
KV_WIDTH = KV_HEADS * HEAD_DIM
Q_WIDTH = HEADS * HEAD_DIM

EPS = 1e-05
THETA = 10000.0
NEGATIVE = -1e30
LANES = 128
F32 = jnp.float32
BF16 = jnp.bfloat16
VMEM_LIMIT = 60 * 1024 * 1024

NN = (((1,), (0,)), ((), ()))
NT = (((1,), (1,)), ((), ()))
TN = (((0,), (0,)), ((), ()))


def dot(a, b, dims=NN):
    return lax.dot_general(a, b, dims, preferred_element_type=F32)


def call(
    kernel,
    name,
    grid,
    in_specs,
    out_specs,
    out_shape,
    scratch=(),
    flops=0,
    bytes_accessed=0,
    after=(),
    vmem=VMEM_LIMIT,
):
    count, more = len(in_specs), len(after)

    def body(info, *refs):
        kernel(info, *refs[:count], *refs[count + more :])

    made = pl.pallas_call(
        body,
        grid_spec=pltpu.PrefetchScalarGridSpec(
            num_scalar_prefetch=1,
            grid=grid,
            in_specs=list(in_specs) + [pl.BlockSpec(memory_space=pl.ANY)] * more,
            out_specs=out_specs,
            scratch_shapes=list(scratch),
        ),
        out_shape=out_shape,
        compiler_params=pltpu.CompilerParams(
            dimension_semantics=("arbitrary",), vmem_limit_bytes=vmem
        ),
        cost_estimate=pl.CostEstimate(
            flops=int(flops), bytes_accessed=int(bytes_accessed), transcendentals=0
        ),
        name=name,
    )
    return lambda *operands: made(*operands, *after)


def per_step(*shape):
    zeros = (0,) * len(shape)
    return pl.BlockSpec((1,) + shape, lambda s, info: (s,) + zeros)


def whole(*shape):
    zeros = (0,) * len(shape)
    return pl.BlockSpec(shape, lambda s, info: zeros, pipeline_mode=pl.Buffered(1))


def kept(*shape):
    zeros = (0,) * len(shape)
    return pl.BlockSpec(shape, lambda s, info: zeros)


def valid_rows(info, slot, block, positions):
    return jnp.clip(info[slot] - block * positions, 0, positions)


def first_bit(count, slots):
    return slots + 1 + count * slots


def together(count, slots):
    return [d for d in range(1, count) if bin(d).count("1") > 1] if count == 4 and slots > 1 else []


def spread_shapes(count, slots):
    joint = together(count, slots)
    return [()] * (slots * (count - len(joint))) + [(slots,)] * len(joint)


def views(refs, count, slots):
    joint = together(count, slots)
    alone = [d for d in range(count) if d not in joint]
    found = {}
    for slot in range(slots):
        for number, distance in enumerate(alone):
            found[slot * count + distance] = refs[slot * len(alone) + number]
        for number, distance in enumerate(joint):
            found[slot * count + distance] = refs[slots * len(alone) + number].at[slot]
    return [found[n] for n in range(count * slots)]


def pick(count, slots, info, in_ref, *refs):
    sems = refs[-1]
    copies = []
    for number, out in enumerate(views(refs[:-1], count, slots)):
        slot, distance = divmod(number, count)
        source = in_ref.at[info[slots + 1 + distance * slots + slot]]
        copies.append(pltpu.make_async_copy(source, out, sems.at[number]))
    for copy in copies:
        copy.start()
    for copy in copies:
        copy.wait()


def put(count, slots, seqs, rows, last, info, *refs):
    out_ref, held, in_sems, out_sems = refs[count:]
    core = info[first_bit(count, slots)]
    for seq in range(seqs):
        place, slot = place_of(info[last + seq], core, count), info[last + seqs + seq]
        for which, row in enumerate(rows):

            @pl.when(place == which)
            def _():
                pltpu.make_async_copy(
                    refs[which].at[row, slot], held.at[seq], in_sems.at[seq]
                ).start()

    copies = [pltpu.make_async_copy(held.at[n], out_ref.at[n], out_sems.at[n]) for n in range(seqs)]
    for seq, copy in enumerate(copies):
        pltpu.make_async_copy(refs[0].at[0, 0], held.at[seq], in_sems.at[seq]).wait()
        copy.start()
    for copy in copies:
        copy.wait()


def rotate(lin, cos, sin, heads, store):
    for head in range(heads):
        low = head * HEAD_DIM
        lead, trail = lin[low : low + HALF], lin[low + HALF : low + HEAD_DIM]
        store(low, (lead * cos - trail * sin).astype(BF16))
        store(low + HALF, (trail * cos + lead * sin).astype(BF16))


def front(positions, count, slots, info, *refs):
    arrays = len(spread_shapes(count, slots))
    x_refs, refs = views(refs[:arrays], count, slots), refs[arrays:]
    gain_ref, wq_ref, wk_t_ref, wv_t_ref, cos_ref, sin_ref = refs[:6]
    all_ref, normed_ref, q_ref, kv_ref, mix_ref, log_ref, stat, acc, x_now = refs[6:]
    slot = pl.program_id(0)
    blk = info[pl.num_programs(0)]
    blocks = lax.div(info[slot] + positions - 1, positions)

    for distance in range(count):
        block = blk ^ distance
        pick_block(x_refs[distance::count], slot, x_now, block < blocks)

        @pl.when(block < blocks)
        def _():
            x = x_now[...].astype(F32)
            all_ref[0, block] = x_now[...]
            normed = (normalised(x)[0] * gain_ref[...]).astype(BF16)
            normed_ref[0, block] = normed
            cos, sin = cos_ref[block], sin_ref[block]

            def store_kv(low, value):
                kv_ref[0, block, low : low + HALF] = value

            rotate(dot(wk_t_ref[...], normed), cos, sin, KV_HEADS, store_kv)
            kv_ref[0, block, KV_WIDTH:] = dot(wv_t_ref[...], normed).astype(BF16)

            def store_q(low, value):
                q_ref[0, block, low : low + HALF] = value

            rotate(dot(wq_ref[...], normed, TN) * (HEAD_DIM**-0.5), cos, sin, HEADS, store_q)

    def visit(block, other, diagonal):
        if diagonal:
            mask = causal_mask(positions, GROUPS)
        lows = [group * HEAD_DIM for group in range(KV_HEADS)]
        keys = [kv_ref[0, other, low : low + HEAD_DIM] for low in lows]
        values = [kv_ref[0, other, KV_WIDTH + low : KV_WIDTH + low + HEAD_DIM] for low in lows]
        asked = [heads_side_by_side(q_ref, block, group) for group in range(KV_HEADS)]
        if not diagonal:
            olds = [stat[group : group + 1] for group in range(KV_HEADS)]
            sums = [stat[KV_HEADS + group : KV_HEADS + group + 1] for group in range(KV_HEADS)]
            accs = [acc[low : low + HEAD_DIM] for low in lows]
        scores = [dot(keys[group], asked[group], TN) for group in range(KV_HEADS)]
        peaks, totals, mixes = [], [], []
        for group in range(KV_HEADS):
            score = scores[group]
            if diagonal:
                score = jnp.where(mask, score, NEGATIVE)
            peak = jnp.max(score, axis=0, keepdims=True)
            if not diagonal:
                peak = jnp.maximum(peak, olds[group])
            weights = jnp.exp(score - peak)
            total = jnp.sum(weights, axis=0, keepdims=True)
            summed = dot(values[group], weights.astype(BF16))
            if not diagonal:
                fade = jnp.exp(olds[group] - peak)
                total = total + sums[group] * fade
                summed = summed + accs[group] * fade
            peaks.append(peak)
            totals.append(total)
            mixes.append(summed)
        for group, low in enumerate(lows):
            stat[group : group + 1] = peaks[group]
            stat[KV_HEADS + group : KV_HEADS + group + 1] = totals[group]
            acc[low : low + HEAD_DIM] = mixes[group]

    def one_block(block, carry):
        visit(block, block, True)

        def one_pair(other, carry):
            visit(block, other, False)
            return carry

        lax.fori_loop(0, block, one_pair, 0)
        log_ref[0, block] = stat[:KV_HEADS] + jnp.log(stat[KV_HEADS:])
        for group in range(KV_HEADS):
            low = group * HEAD_DIM
            share = 1.0 / stat[KV_HEADS + group : KV_HEADS + group + 1]
            mix = (acc[low : low + HEAD_DIM] * share).astype(BF16)
            for place in range(GROUPS):
                row = (group * GROUPS + place) * HEAD_DIM
                mix_ref[0, block, row : row + HEAD_DIM] = mix[
                    :, place * positions : (place + 1) * positions
                ]
        return carry

    lax.fori_loop(0, blocks, one_block, 0)


def causal_mask(positions, copies):
    keys = lax.broadcasted_iota(jnp.int32, (positions, positions), 0)
    queries = lax.broadcasted_iota(jnp.int32, (positions, positions), 1)
    return jnp.concatenate([keys <= queries] * copies, 1)


def heads_side_by_side(ref, block, group):
    first = group * GROUPS * HEAD_DIM
    return jnp.concatenate(
        [ref[0, block, first + p * HEAD_DIM : first + (p + 1) * HEAD_DIM] for p in range(GROUPS)],
        1,
    )


def pieces_of(columns):
    return [(start, min(LANES, columns - start)) for start in range(0, columns, LANES)]


def place_of(distance, core, count):
    if count == 4:
        return distance ^ (3 * (((distance ^ (distance >> 1)) & 1) * core))
    return distance


class Parts:
    def __init__(self, halves, outs, sems, count, blk):
        self.halves, self.outs, self.sems, self.count, self.blk = halves, outs, sems, count, blk
        self.size = halves[0].shape[0] // count
        self.copies = []

    def write(self, row, value):
        done, rows = 0, value.shape[0]
        while done < rows:
            number, inside = divmod(row + done, self.size)
            take = min(self.size - inside, rows - done)
            half, part = divmod(number, self.count)
            place = place_of(part ^ self.blk, half, self.count)
            start = pl.multiple_of(place * self.size + inside, 16)
            self.halves[half][pl.ds(start, take)] = value[done : done + take]
            done += take
            if inside + take == self.size:
                whole_part = pl.ds(pl.multiple_of(place * self.size, 16), self.size)
                copy = pltpu.make_async_copy(
                    self.halves[half].at[whole_part],
                    self.outs[half].at[whole_part],
                    self.sems.at[number],
                )
                copy.start()
                self.copies.append(copy)


def pack_into(parts, row, acc):
    rows, columns = acc.shape
    for start, width in pieces_of(columns):
        part = acc[:, start : start + width].astype(BF16)
        if width < LANES:
            half = rows // 2
            part = jnp.concatenate([part[:half], part[half:]], 1)
        parts.write(row, part)
        row += part.shape[0]
    return row


def gain_rows(acc):
    ones = jnp.ones((16, acc.shape[1]), BF16)
    sums = dot(ones, acc[...].astype(BF16), NT)[:1]
    parts = [sums[:, start : start + width] for start, width in pieces_of(sums.shape[1])]
    short = LANES - parts[-1].shape[1]
    if short:
        parts[-1] = jnp.concatenate([parts[-1], jnp.zeros((1, short), F32)], 1)
    return parts


def pack_all(info, bit_at, count, blk, buffers, outs, sems, accs, last=None):
    def fill(halves, outs):
        parts = Parts(halves, outs, sems, count, blk)
        row = 0
        for acc in accs:
            row = pack_into(parts, row, acc)
        if last is not None:
            parts.write(row, last)
            row += last.shape[0]
        rest = 2 * halves[0].shape[0] - row
        if rest:
            parts.write(row, jnp.zeros((rest, LANES), BF16))
        for copy in parts.copies:
            copy.wait()

    (mine, send), (mine_out, send_out) = buffers, outs
    pl.when(info[bit_at] == 0)(lambda: fill((mine, send), (mine_out, send_out)))
    pl.when(info[bit_at] != 0)(lambda: fill((send, mine), (send_out, mine_out)))


def packed_rows(rows, columns):
    return rows * columns // LANES


def pick_block(refs, distance, out_ref, wanted):
    for which, ref in enumerate(refs):

        @pl.when(jnp.logical_and(wanted, distance == which))
        def _():
            out_ref[...] = ref[...]


def place_groups(count):
    return [[0, 2], [1, 3]] if count == 4 else [[place] for place in range(count)]


def place_block(refs, count, place, value_ref):
    for ref, group in zip(refs, place_groups(count)):
        inside = functools.reduce(jnp.logical_or, [place == member for member in group])

        @pl.when(inside)
        def _():
            ref[0, 0] = value_ref[...]


def normalised(value):
    scaled = lax.rsqrt(jnp.mean(value * value, axis=0, keepdims=True) + EPS)
    return value * scaled, scaled


def norm_back(upstream, gain, normal, scaled):
    inner = upstream * gain
    return scaled * (inner - normal * jnp.mean(inner * normal, axis=0, keepdims=True))


def valid_lanes(rows, positions):
    lane = lax.broadcasted_iota(jnp.int32, (1, positions), 1)
    return (lane < rows).astype(F32)


def feed_forward(positions, chunk, count, slots, info, *refs):
    arrays = 1 + len(spread_shapes(count, slots))
    x_ref, cot_refs, refs = refs[0], views(refs[1:arrays], count, slots), refs[arrays:]
    mix_ref, gain_ref = refs[:2]
    far_weights = refs[2:6]
    groups = len(place_groups(count))
    out_refs, refs = refs[6 : 6 + groups], refs[6 + groups :]
    mid_ref, gattn_ref, delta_ref, mine_ref, send_ref, gain_sum_ref = refs[:6]
    acc_gate, acc_up, acc_down, acc_out, cot_now, out_now = refs[6:12]
    wo_ref, wg_ref, wu_ref, wd_t_ref = refs[12:16]
    buffers, weight_sems, part_sems = refs[16:18], refs[18], refs[19]
    step = pl.program_id(0)
    place, slot = lax.div(step, slots), lax.rem(step, slots)
    distance = place_of(place, info[first_bit(count, slots)], count)
    rows = valid_rows(info, slot, info[slots] ^ distance, positions)
    width = cot_now.shape[0]
    hidden_width = wg_ref.shape[1]

    everything = slice(None)
    pieces = [("first", 0, (everything, everything))]
    for start in range(0, hidden_width, chunk):
        part = slice(start, start + chunk)
        pieces += [(start, number, (everything, part)) for number in (1, 2, 3)]
    fetches = {}
    for number, (when, weight, where) in enumerate(pieces):
        copy = pltpu.make_async_copy(
            far_weights[weight].at[where], refs[12 + weight].at[where], weight_sems.at[number]
        )
        fetches.setdefault(when, []).append(copy)

    @pl.when(step == 0)
    def _():
        for copies in fetches.values():
            for copy in copies:
                copy.start()
        for acc in (acc_gate, acc_up, acc_down, acc_out, gain_sum_ref):
            acc[...] = jnp.zeros_like(acc)

    @pl.when(jnp.logical_and(rows <= 0, step == 0))
    def _():
        for copies in fetches.values():
            for copy in copies:
                copy.wait()

    @pl.when(rows <= 0)
    def _():
        out_now[...] = jnp.zeros_like(out_now)

    pick_block(cot_refs, slot * count + distance, cot_now, rows > 0)

    def work(need):
        need("first")
        valid = valid_lanes(rows, positions)
        mix = mix_ref[0, 0]
        middle = x_ref[0, 0].astype(F32) + dot(wo_ref[...], mix, TN)
        normal, scaled = normalised(middle)
        gain = gain_ref[...]
        normed = (normal * gain).astype(BF16)
        grad_y = cot_now[...].astype(F32) * valid
        grad_low = grad_y.astype(BF16)
        branch = jnp.zeros((width, positions), F32)
        grad_normed = jnp.zeros((width, positions), F32)
        for start in range(0, hidden_width, chunk):
            part = slice(start, start + chunk)
            need(start)
            gate = dot(wg_ref[:, part], normed, TN)
            up = dot(wu_ref[:, part], normed, TN)
            grad_hidden = dot(wd_t_ref[:, part], grad_low, TN)
            sig = 1.0 / (1.0 + jnp.exp(-gate))
            act = gate * sig
            hidden = (act * up).astype(BF16)
            grad_gate = (grad_hidden * up * (sig * (1.0 + gate * (1.0 - sig)))).astype(BF16)
            grad_up = (grad_hidden * act).astype(BF16)
            branch = branch + dot(wd_t_ref[:, part], hidden)
            grad_normed = grad_normed + dot(wg_ref[:, part], grad_gate)
            grad_normed = grad_normed + dot(wu_ref[:, part], grad_up)
            acc_down[:, part] += dot(grad_low, hidden, NT)
            acc_gate[:, part] += dot(normed, grad_gate, NT)
            acc_up[:, part] += dot(normed, grad_up, NT)
        out_now[...] = (valid * (middle + branch)).astype(BF16)
        gain_sum_ref[...] += grad_normed * normal
        grad_middle = grad_y + norm_back(grad_normed, gain, normal, scaled)
        grad_mid_low = grad_middle.astype(BF16)
        mid_ref[0, 0] = grad_mid_low
        acc_out[...] += dot(mix, grad_mid_low, NT)
        grad_attn = dot(wo_ref[...], grad_mid_low).astype(BF16)
        gattn_ref[0, 0] = grad_attn
        product = grad_attn.astype(F32) * mix.astype(F32)
        for head in range(HEADS):
            part = slice(head * HEAD_DIM, (head + 1) * HEAD_DIM)
            group, turn = head // GROUPS, head % GROUPS
            lanes = slice(turn * positions, (turn + 1) * positions)
            delta_ref[0, 0, group : group + 1, lanes] = jnp.sum(
                product[part], axis=0, keepdims=True
            )

    def wait_for(when):
        for copy in fetches[when]:
            copy.wait()

    pl.when(jnp.logical_and(rows > 0, step == 0))(lambda: work(wait_for))
    pl.when(jnp.logical_and(rows > 0, step > 0))(lambda: work(lambda when: None))

    place_block(out_refs, count, place, out_now)

    @pl.when(step == count * slots - 1)
    def _():
        pack_all(
            info,
            first_bit(count, slots),
            count,
            info[slots],
            buffers,
            (mine_ref, send_ref),
            part_sems,
            (acc_gate, acc_up, acc_down, acc_out),
        )


def rotate_back(value, cos, sin, heads):
    parts = []
    for head in range(heads):
        low = head * HEAD_DIM
        lead, trail = value[low : low + HALF], value[low + HALF : low + HEAD_DIM]
        parts += [lead * cos + trail * sin, trail * cos - lead * sin]
    return jnp.concatenate(parts, 0)


def attend_back(positions, count, info, *refs):
    q_ref, kv_ref, gattn_ref, log_ref, delta_ref, cos_ref, sin_ref = refs[:7]
    lin_ref, dq, dkv = refs[7:]
    blocks = lax.div(info[pl.program_id(0)] + positions - 1, positions)

    def visit(block, other, diagonal):
        if diagonal:
            mask = causal_mask(positions, GROUPS)
        lows = [group * HEAD_DIM for group in range(KV_HEADS)]
        keys = [kv_ref[0, other, low : low + HEAD_DIM] for low in lows]
        values = [kv_ref[0, other, KV_WIDTH + low : KV_WIDTH + low + HEAD_DIM] for low in lows]
        asked = [heads_side_by_side(q_ref, block, group) for group in range(KV_HEADS)]
        grads = [heads_side_by_side(gattn_ref, block, group) for group in range(KV_HEADS)]
        logs = [log_ref[0, block, group : group + 1] for group in range(KV_HEADS)]
        deltas = [delta_ref[0, block, group : group + 1] for group in range(KV_HEADS)]
        results = []
        for group in range(KV_HEADS):
            scores = dot(keys[group], asked[group], TN)
            grad_probs = dot(values[group], grads[group], TN)
            probs = jnp.exp(scores - logs[group])
            if diagonal:
                probs = jnp.where(mask, probs, 0.0)
            grad_scores = (probs * (grad_probs - deltas[group])).astype(BF16)
            grad_value = dot(grads[group], probs.astype(BF16), NT)
            grad_query = dot(keys[group], grad_scores)
            grad_key = dot(asked[group], grad_scores, NT)
            results.append((grad_query, grad_key, grad_value))
        for low, (grad_query, grad_key, grad_value) in zip(lows, results):
            rows = slice(low, low + HEAD_DIM)
            more = slice(KV_WIDTH + low, KV_WIDTH + low + HEAD_DIM)
            if diagonal:
                dq[rows] = grad_query
                dkv[other, rows] = grad_key
                dkv[other, more] = grad_value
            else:
                dq[rows] += grad_query
                dkv[other, rows] += grad_key
                dkv[other, more] += grad_value

    def one_block(block, carry):
        visit(block, block, True)

        def one_pair(other, carry):
            visit(block, other, False)
            return carry

        lax.fori_loop(0, block, one_pair, 0)
        grad = jnp.concatenate(
            [
                dq[
                    (head // GROUPS) * HEAD_DIM : (head // GROUPS + 1) * HEAD_DIM,
                    (head % GROUPS) * positions : (head % GROUPS + 1) * positions,
                ]
                for head in range(HEADS)
            ],
            0,
        ) * (HEAD_DIM**-0.5)
        lin = rotate_back(grad, cos_ref[block], sin_ref[block], HEADS)
        lin_ref[0, block, :Q_WIDTH] = lin.astype(BF16)
        return carry

    lax.fori_loop(0, blocks, one_block, 0)

    def one_rotation(block, carry):
        grad = dkv[block]
        rotated = rotate_back(grad[:KV_WIDTH], cos_ref[block], sin_ref[block], KV_HEADS)
        lin_ref[0, block, Q_WIDTH : Q_WIDTH + KV_WIDTH] = rotated.astype(BF16)
        lin_ref[0, block, Q_WIDTH + KV_WIDTH :] = grad[KV_WIDTH:].astype(BF16)
        return carry

    lax.fori_loop(0, blocks, one_rotation, 0)


def project_back(positions, count, slots, info, *refs):
    x_ref, refs = refs[0], refs[1:]
    gain_ref, normed_ref, lin_ref, mid_ref, wq_ref, wk_t_ref, wv_t_ref, other_gain_ref = refs[:8]
    groups = len(place_groups(count))
    out_refs, refs = refs[8 : 8 + groups], refs[8 + groups :]
    mine_ref, send_ref, gain_sum, acc_q, acc_k, acc_v, out_now = refs[:7]
    buffers, part_sems = refs[7:9], refs[9]
    step = pl.program_id(0)
    place, slot = lax.div(step, slots), lax.rem(step, slots)
    distance = place_of(place, info[first_bit(count, slots)], count)
    blk = info[slots]
    rows = valid_rows(info, slot, blk ^ distance, positions)

    @pl.when(step == 0)
    def _():
        for acc in (acc_q, acc_k, acc_v, gain_sum):
            acc[...] = jnp.zeros_like(acc)


    @pl.when(rows <= 0)
    def _():
        out_now[...] = jnp.zeros_like(out_now)

    @pl.when(rows > 0)
    def _():
        lin = lin_ref[0, 0]
        normed = normed_ref[0, 0]
        acc_q[...] += dot(normed, lin[:Q_WIDTH], NT)
        acc_k[...] += dot(lin[Q_WIDTH : Q_WIDTH + KV_WIDTH], normed, NT)
        acc_v[...] += dot(lin[Q_WIDTH + KV_WIDTH :], normed, NT)
        grad_normed = dot(wq_ref[...], lin[:Q_WIDTH])
        grad_normed += dot(wk_t_ref[...], lin[Q_WIDTH : Q_WIDTH + KV_WIDTH], TN)
        grad_normed += dot(wv_t_ref[...], lin[Q_WIDTH + KV_WIDTH :], TN)
        normal, scaled = normalised(x_ref[0, 0].astype(F32))
        gain_sum[...] += grad_normed * normal
        back = norm_back(grad_normed, gain_ref[...], normal, scaled)
        out_now[...] = (mid_ref[0, 0].astype(F32) + back).astype(BF16)

    place_block(out_refs, count, place, out_now)

    @pl.when(step == count * slots - 1)
    def _():
        gains = gain_rows(gain_sum) + gain_rows(other_gain_ref)
        gains.append(jnp.zeros((-len(gains) % 16, LANES), F32))
        gains = jnp.concatenate(gains, 0).astype(BF16)
        pack_all(
            info,
            first_bit(count, slots),
            count,
            blk,
            buffers,
            (mine_ref, send_ref),
            part_sems,
            (acc_q, acc_k, acc_v),
            gains,
        )


def unpack(count, slots, jobs, info, *refs):
    refs = list(refs)
    take = lambda number: [refs.pop(0) for _ in range(number)]
    core, turn = info[first_bit(count, slots)], info[first_bit(count, slots) + 1]
    sources = [take(count), take(count)]
    outs = [take(len(shapes)) for shapes, *_ in jobs]
    gains = [take(2 if gain_width else 0) for _, _, gain_width, _, _ in jobs]
    buffers = take(len(jobs))
    stages = [take(len(shapes)) for shapes, *_ in jobs]
    in_sems, out_sems = take(2)
    arrivals, number = [], 0
    for (_, shares, _, base, size), buffer in zip(jobs, buffers):
        copies = []
        piece = size // shares
        for which in range(2):
            for place in range(count):
                distance = place_of(place, core ^ which, count)
                part = (core ^ which) * count + (info[slots] ^ distance)
                for share in range(shares):
                    moved = share if shares == 1 else turn ^ share
                    start = pl.multiple_of(part * size + moved * piece, 16)
                    copies.append(
                        pltpu.make_async_copy(
                            sources[which][place].at[pl.ds(base + share * piece, piece)],
                            buffer.at[pl.ds(start, piece)],
                            in_sems.at[number],
                        )
                    )
                    number += 1
        arrivals.append(copies)
    for copies in arrivals:
        for copy in copies:
            copy.start()
    leaving, number = [], 0
    for job, (shapes, _, gain_width, _, _) in enumerate(jobs):
        buffer, row = buffers[job], 0
        for copy in arrivals[job]:
            copy.wait()
        for out, stage, (rows, columns) in zip(outs[job], stages[job], shapes):
            for first, width in pieces_of(columns):
                if width == LANES:
                    stage[:, first : first + LANES] = buffer[row : row + rows].astype(F32)
                    row += rows
                else:
                    half = rows // 2
                    part = buffer[row : row + half].astype(F32)
                    stage[:half, first : first + width] = part[:, :width]
                    stage[half:, first : first + width] = part[:, width:]
                    row += half
            copy = pltpu.make_async_copy(stage, out, out_sems.at[number])
            copy.start()
            leaving.append(copy)
            number += 1
        if gain_width:
            sums, line = buffer[row : row + 16].astype(F32), 0
            for ref in gains[job]:
                for first, width in pieces_of(gain_width):
                    ref[first : first + width] = sums[line, :width]
                    line += 1
    for copy in leaving:
        copy.wait()


def added(arrays):
    total = arrays[0].astype(F32)
    for array in arrays[1:]:
        total = total + array.astype(F32)
    return total.astype(BF16)


def bits_of(count):
    return count.bit_length() - 1


def later(value, *others):
    return lax.optimization_barrier((value, others))[0]


class Sum:
    def __init__(self, blk_count, batch_count):
        self.blk_count, self.rest_count = blk_count, batch_count // 2
        self.rest = lax.axis_index("batch") // 2
        self.bits = bits_of(self.rest_count)

    def swap_cores(self, array):
        pairs = [(i, i ^ 1) for i in range(2 * self.rest_count)]
        return lax.ppermute(array, "batch", pairs)

    def over_blk(self, array, distance):
        return lax.ppermute(array, "blk", [(i, i ^ distance) for i in range(self.blk_count)])

    def over_rest(self, array, bit):
        pairs = [(i, i ^ (2 << bit)) for i in range(2 * self.rest_count)]
        return lax.ppermute(array, "batch", pairs)

    def along(self, array, even, odd):
        pairs = []
        for blk in range(self.blk_count):
            for batch in range(2 * self.rest_count):
                to_blk = blk ^ (odd if batch % 2 else even)
                pairs.append(
                    (blk * 2 * self.rest_count + batch, to_blk * 2 * self.rest_count + batch)
                )
        return lax.ppermute(array, ("blk", "batch"), pairs)

    def reversed_rest(self):
        bits = [((self.rest >> k) & 1) << (self.bits - 1 - k) for k in range(self.bits)]
        return functools.reduce(lambda a, b: a | b, bits, jnp.int32(0))

    def parts_of_chip(self, mine, send):
        got = self.swap_cores(send)
        pieces = 2 if self.blk_count == 4 else self.blk_count
        size = mine.shape[0] // pieces
        return [
            added([array[n * size : (n + 1) * size] for array in (mine, got)])
            for n in range(pieces)
        ]

    def first_hop(self, parts):
        if self.blk_count == 4:
            return [parts[0], self.along(parts[1], 2, 1)]
        return [parts[0]] + [self.over_blk(parts[d], d) for d in range(1, self.blk_count)]

    def second_hop(self, arrays):
        if self.blk_count == 4:
            size = arrays[0].shape[0] // 2
            own = added([array[:size] for array in arrays])
            return [own, self.along(added([array[size:] for array in arrays]), 1, 2)]
        return arrays

    def send_half(self, arrays, k):
        half = arrays[0].shape[0] // 2
        side = (self.rest >> k) & 1

        def cut(which):
            return added([lax.dynamic_slice_in_dim(a, which * half, half, 0) for a in arrays])

        return [cut(side), self.over_rest(cut(1 - side), k)]

    def reduce_rest(self, arrays):
        for k in range(self.bits):
            arrays = self.send_half(arrays, k)
        return added(arrays)

    def gather_rest(self, share):
        block = share
        for k in reversed(range(1, self.bits)):
            block = jnp.concatenate([block, self.over_rest(block, k)], 0)
        return block, self.over_rest(block, 0)

    def reduce_rest_small(self, piece):
        for k in range(self.bits):
            piece = added([piece, self.over_rest(piece, k)])
        return piece

    def gather_blk(self, piece):
        if self.blk_count == 4:
            one, two = self.along(piece, 1, 2), self.along(piece, 2, 1)
            own = [piece, one, two, self.along(later(one, two), 2, 1)]
        else:
            own = [piece] + [self.over_blk(piece, d) for d in range(1, self.blk_count)]
        return own, [self.swap_cores(part) for part in own]


def on_device(
    blk_count,
    batch_count,
    hidden_in,
    lengths,
    attn_gain,
    w_query,
    w_key,
    w_value,
    w_output,
    mlp_gain,
    w_gate,
    w_up,
    w_down,
    cotangent,
):
    seqs, positions, width = hidden_in.shape
    ff = w_gate.shape[1]
    count = blk_count
    devices = blk_count * batch_count
    slots = -(-seqs // count)
    wide = GROUPS * positions
    blk = lax.axis_index("blk")
    x_t = jnp.swapaxes(hidden_in, 1, 2)
    cot_t = jnp.swapaxes(cotangent, 1, 2)

    numbers = jnp.arange(seqs, dtype=jnp.int32)
    ahead = (lengths[None, :] > lengths[:, None]) | (
        (lengths[None, :] == lengths[:, None]) & (numbers[None, :] < numbers[:, None])
    )
    rank = jnp.sum(ahead.astype(jnp.int32), 1)
    slot_of, place = rank // count, rank % count
    batch = lax.axis_index("batch")
    owner = jnp.where((slot_of + batch) % 2 == 0, place, count - 1 - place)
    wanted_device = blk ^ jnp.repeat(jnp.arange(count, dtype=jnp.int32), slots)
    wanted_slot = jnp.tile(jnp.arange(slots, dtype=jnp.int32), count)
    match = (
        (owner[None, :] == wanted_device[:, None]) & (slot_of[None, :] == wanted_slot[:, None])
    ).astype(jnp.int32)
    sequence = jnp.sum(match * numbers[None, :], 1)
    own_lengths = jnp.sum(match[:slots] * lengths[None, :], 1)
    total = Sum(blk_count, batch_count)
    info = jnp.concatenate(
        [own_lengths, jnp.stack([blk]), sequence, jnp.stack([batch % 2, total.reversed_rest()])]
        + [owner ^ blk, slot_of]
    ).astype(jnp.int32)
    bit_at = first_bit(count, slots)

    frequency = np.float32(THETA) ** (
        -np.arange(HALF, dtype=np.float32) * np.float32(2.0) / np.float32(HEAD_DIM)
    )
    places = np.arange(count * positions, dtype=np.float32).reshape(count, 1, positions)
    angles = (frequency[None, :, None] * places).astype(np.float32)
    cos_table, sin_table = jnp.asarray(np.cos(angles)), jnp.asarray(np.sin(angles))
    gain_first = attn_gain.astype(F32)[:, None]
    gain_second = mlp_gain.astype(F32)[:, None]
    anywhere = pl.BlockSpec(memory_space=pl.ANY)

    def spread(array, name, after=None):
        picked = call(
            functools.partial(pick, count, slots),
            name,
            (1,),
            [whole(seqs, width, positions)],
            [anywhere] * len(spread_shapes(count, slots)),
            [
                jax.ShapeDtypeStruct(shape + (width, positions), BF16)
                for shape in spread_shapes(count, slots)
            ],
            [pltpu.SemaphoreType.DMA((count * slots,))],
        )(info, array)
        if after is not None:
            picked = later(picked, after)
        joint = together(count, slots)
        alone = [d for d in range(count) if d not in joint]
        got = []
        for slot in range(slots):
            held = min(count, seqs - slot * count)
            for distance in alone:
                if distance == 0:
                    got.append(picked[len(got)])
                    continue
                pairs = []
                for source in range(count):
                    for other in range(batch_count):
                        target = source ^ distance
                        turn = target if (slot + other) % 2 == 0 else count - 1 - target
                        if turn < held:
                            pairs.append(
                                (source * batch_count + other, target * batch_count + other)
                            )
                got.append(lax.ppermute(picked[len(got)], ("blk", "batch"), pairs))
        for distance in joint:
            got.append(total.over_blk(picked[len(got)], distance))
        return got

    def place_at(info, place):
        return place_of(place, info[bit_at], count)

    def first_back(parts):
        if count == 4:
            return [(parts[0], 0), (parts[0], 1)], total.along(parts[1], 1, 2)
        got = [(parts[0], 0)]
        for distance in range(1, count):
            got.append((total.over_blk(parts[distance], distance), 0))
        return got, None

    def second_back(got, came):
        if count == 4:
            sent = jnp.concatenate([got[1][0][1:], came[1:]], 0)
            final = total.along(sent, 2, 1)
            return [got[0], (came, 0), (final, 0), (final, 1)]
        return got

    def collect(got, name):
        last = bit_at + 2

        return call(
            functools.partial(put, count, slots, seqs, [row for _, row in got], last),
            name,
            (1,),
            [anywhere] * count,
            anywhere,
            jax.ShapeDtypeStruct((seqs, width, positions), BF16),
            [pltpu.VMEM((seqs, width, positions), BF16)]
            + [pltpu.SemaphoreType.DMA((seqs,))] * 2,
        )(info, *[array for array, _ in got])

    spread_specs = [whole(*shape, width, positions) for shape in spread_shapes(count, slots)]
    x_moved = spread(x_t, "pick_hidden")
    cot_moved = spread(cot_t, "pick_cotangent")

    table = whole(count, HALF, positions)
    blocks_of = lambda rows: per_step(count, rows, positions)
    unit_flops = 4 * slots * count * positions * positions * HEADS * 256
    dense = 2 * slots * count * positions * width
    x_all, normed, queries, kv, mix, log_total = call(
        functools.partial(front, positions, count, slots),
        "front",
        (slots,),
        spread_specs
        + [whole(width, 1), whole(width, Q_WIDTH)]
        + [whole(KV_WIDTH, width)] * 2
        + [table, table],
        [
            blocks_of(width),
            blocks_of(width),
            blocks_of(Q_WIDTH),
            blocks_of(2 * KV_WIDTH),
            blocks_of(Q_WIDTH),
            per_step(count, KV_HEADS, wide),
        ],
        [
            jax.ShapeDtypeStruct((slots, count, width, positions), BF16),
            jax.ShapeDtypeStruct((slots, count, width, positions), BF16),
            jax.ShapeDtypeStruct((slots, count, Q_WIDTH, positions), BF16),
            jax.ShapeDtypeStruct((slots, count, 2 * KV_WIDTH, positions), BF16),
            jax.ShapeDtypeStruct((slots, count, Q_WIDTH, positions), BF16),
            jax.ShapeDtypeStruct((slots, count, KV_HEADS, wide), F32),
        ],
        [
            pltpu.VMEM((2 * KV_HEADS, wide), F32),
            pltpu.VMEM((KV_WIDTH, wide), F32),
            pltpu.VMEM((width, positions), BF16),
        ],
        flops=dense * 960 + 2 * unit_flops,
    )(
        info,
        *x_moved,
        gain_first,
        w_query,
        w_key.T,
        w_value.T,
        cos_table,
        sin_table,
    )

    first_shapes = [(width, ff), (width, ff), (width, ff), (Q_WIDTH, width)]
    first_rows = sum(packed_rows(*shape) for shape in first_shapes)
    unit = 16 * devices
    first_half = -(-first_rows // unit) * unit // 2

    def leaving(group):
        def where(step, info):
            now, slot = lax.div(step, slots), lax.rem(step, slots)
            row, at = 0, jnp.where(now < group[0], 0, slots - 1)
            for number, member in enumerate(group):
                row = jnp.where(now >= member, number, row)
                at = jnp.where(now == member, slot, at)
            return (row, at, 0, 0)

        return pl.BlockSpec((1, 1, width, positions), where)

    def block_spec(*shape):
        zeros = (0,) * len(shape)

        def where(step, info):
            place = lax.div(step, slots)
            return (lax.rem(step, slots), info[slots] ^ place_at(info, place)) + zeros

        return pl.BlockSpec((1, 1) + shape, where)

    leavings = [leaving(group) for group in place_groups(count)]
    left = [
        jax.ShapeDtypeStruct((len(group), slots, width, positions), BF16)
        for group in place_groups(count)
    ]
    *layer_t, grad_middle, grad_attn, deltas, mine_first, send_first, gain_sum = call(
        functools.partial(feed_forward, positions, 512, count, slots),
        "feed_forward",
        (slots * count,),
        [block_spec(width, positions)]
        + spread_specs
        + [
            block_spec(Q_WIDTH, positions),
            whole(width, 1),
        ]
        + [anywhere] * 4,
        leavings
        + [
            block_spec(width, positions),
            block_spec(Q_WIDTH, positions),
            block_spec(KV_HEADS, wide),
            anywhere,
            anywhere,
            kept(width, positions),
        ],
        left
        + [
            jax.ShapeDtypeStruct((slots, count, width, positions), BF16),
            jax.ShapeDtypeStruct((slots, count, Q_WIDTH, positions), BF16),
            jax.ShapeDtypeStruct((slots, count, KV_HEADS, wide), F32),
            jax.ShapeDtypeStruct((first_half, LANES), BF16),
            jax.ShapeDtypeStruct((first_half, LANES), BF16),
            jax.ShapeDtypeStruct((width, positions), F32),
        ],
        [pltpu.VMEM(shape, F32) for shape in first_shapes]
        + [pltpu.VMEM((width, positions), BF16)] * 2
        + [pltpu.VMEM((Q_WIDTH, width), BF16)]
        + [pltpu.VMEM((width, ff), BF16)] * 3
        + [pltpu.VMEM((first_half, LANES), BF16)] * 2
        + [
            pltpu.SemaphoreType.DMA((1 + 3 * (ff // 512),)),
            pltpu.SemaphoreType.DMA((2 * count,)),
        ],
        flops=9 * dense * ff,
    )(
        info,
        x_all,
        *cot_moved,
        mix,
        gain_second,
        w_output,
        w_gate,
        w_up,
        w_down.T,
    )

    parts_first = total.parts_of_chip(mine_first, send_first)

    second_shapes = [(width, Q_WIDTH), (KV_WIDTH, width), (KV_WIDTH, width)]
    second_rows = sum(packed_rows(*shape) for shape in second_shapes)
    second_rows += -(-2 * len(pieces_of(width)) // 16) * 16
    second_half = -(-second_rows // unit) * unit // 2
    lin_width = Q_WIDTH + 2 * KV_WIDTH
    grad_lin = call(
        functools.partial(attend_back, positions, count),
        "attend_back",
        (slots,),
        [
            blocks_of(Q_WIDTH),
            blocks_of(2 * KV_WIDTH),
            blocks_of(Q_WIDTH),
            per_step(count, KV_HEADS, wide),
            per_step(count, KV_HEADS, wide),
            table,
            table,
        ],
        blocks_of(lin_width),
        jax.ShapeDtypeStruct((slots, count, lin_width, positions), BF16),
        [
            pltpu.VMEM((KV_WIDTH, wide), F32),
            pltpu.VMEM((count, 2 * KV_WIDTH, positions), F32),
        ],
        flops=5 * unit_flops,
        after=[parts_first[0]],
    )(info, queries, kv, grad_attn, log_total, deltas, cos_table, sin_table)

    layer_got, layer_came = first_back(layer_t)
    hop_first = total.first_hop(parts_first)
    hop_first, layer_came = later((hop_first, layer_came), grad_lin)
    hop_first = total.second_hop(hop_first)
    layer_got = second_back(layer_got, layer_came)

    *grad_in_t, mine_second, send_second = call(
        functools.partial(project_back, positions, count, slots),
        "project_back",
        (slots * count,),
        [
            block_spec(width, positions),
            whole(width, 1),
            block_spec(width, positions),
            block_spec(lin_width, positions),
            block_spec(width, positions),
            whole(width, Q_WIDTH),
            whole(KV_WIDTH, width),
            whole(KV_WIDTH, width),
            whole(width, positions),
        ],
        leavings + [anywhere, anywhere],
        left
        + [
            jax.ShapeDtypeStruct((second_half, LANES), BF16),
            jax.ShapeDtypeStruct((second_half, LANES), BF16),
        ],
        [
            pltpu.VMEM((width, positions), F32),
            pltpu.VMEM((width, Q_WIDTH), F32),
            pltpu.VMEM((KV_WIDTH, width), F32),
            pltpu.VMEM((KV_WIDTH, width), F32),
        ]
        + [pltpu.VMEM((width, positions), BF16)]
        + [pltpu.VMEM((second_half, LANES), BF16)] * 2
        + [pltpu.SemaphoreType.DMA((2 * count,))],
        flops=2 * dense * 960,
        after=[hop_first[0]],
    )(
        info,
        x_all,
        gain_first,
        normed,
        grad_lin,
        grad_middle,
        w_query,
        w_key.T,
        w_value.T,
        gain_sum,
    )
    def tied(got, *others):
        return [(later(array, *others), row) for array, row in got]

    arrays = [array for array, _ in layer_got]
    hop_first, arrays = later((hop_first, arrays), mine_second)
    half_first = total.send_half(hop_first, 0)
    arrays, send_second, grad_in_t = later((arrays, send_second, grad_in_t), half_first[0])
    layer_got = [(array, row) for array, (_, row) in zip(arrays, layer_got)]
    layer_out = collect(layer_got, "put_layer")
    grad_got, grad_came = first_back(grad_in_t)
    half_first = later(half_first, layer_out)
    for k in range(1, total.bits):
        half_first = total.send_half(half_first, k)
    grad_got = second_back(grad_got, grad_came)
    parts_second = total.parts_of_chip(mine_second, send_second)
    piece_second = added(total.second_hop(total.first_hop(parts_second)))
    share = added(half_first)
    block, came = total.gather_rest(share)
    grad_in = collect(tied(grad_got, block), "put_grad")
    piece_second = total.reduce_rest_small(piece_second)
    size_first, size_second = 2 * block.shape[0], piece_second.shape[0]
    piece = jnp.concatenate([block, later(came, grad_in), piece_second], 0)
    own, other = total.gather_blk(piece)
    shares = batch_count // 2
    jobs = [
        (second_shapes, 1, width, size_first, size_second),
        (first_shapes, shares, 0, 0, size_first),
    ]
    results = second_shapes + first_shapes
    g_query, g_key_t, g_value_t, g_gate, g_up, g_down_t, g_out, gain_one, gain_two = call(
        functools.partial(unpack, count, slots, jobs),
        "unpack",
        (1,),
        [anywhere] * (2 * count),
        [anywhere] * len(results) + [kept(width)] * 2,
        [jax.ShapeDtypeStruct(shape, F32) for shape in results]
        + [jax.ShapeDtypeStruct((width,), F32)] * 2,
        [
            pltpu.VMEM((2 * count * size_second, LANES), BF16),
            pltpu.VMEM((2 * count * size_first, LANES), BF16),
        ]
        + [pltpu.VMEM(shape, F32) for shape in results]
        + [
            pltpu.SemaphoreType.DMA((2 * count * (1 + shares),)),
            pltpu.SemaphoreType.DMA((len(results),)),
        ],
        bytes_accessed=12 * count * size_first * LANES,
    )(info, *own, *other)
    return (
        jnp.swapaxes(layer_out, 1, 2),
        jnp.swapaxes(grad_in, 1, 2),
        gain_one,
        g_query,
        g_key_t.T,
        g_value_t.T,
        g_out,
        gain_two,
        g_gate,
        g_up,
        g_down_t.T,
    )


def solution(mesh):
    rows = P("batch", "blk", None)
    return jax.shard_map(
        functools.partial(on_device, mesh.shape["blk"], mesh.shape["batch"]),
        mesh=mesh,
        in_specs=(rows, P("batch")) + (P(),) * 9 + (rows,),
        out_specs=(rows, rows) + (P(),) * 9,
        check_vma=False,
    )
```

```python
import functools

import jax
import jax.numpy as jnp
import numpy as np
from jax import lax
from jax.experimental import pallas as pl
from jax.experimental.pallas import tpu as pltpu
from jax.sharding import PartitionSpec as P

HEADS = 9
KV_HEADS = 3
HEAD_DIM = 64
GROUPS = HEADS // KV_HEADS
HALF = HEAD_DIM // 2
KV_WIDTH = KV_HEADS * HEAD_DIM
Q_WIDTH = HEADS * HEAD_DIM

EPS = 1e-05
THETA = 10000.0
NEGATIVE = -1e30
LANES = 128
F32 = jnp.float32
BF16 = jnp.bfloat16
VMEM_MIB = {"pick": 8, "front": 32, "feed": 44, "attend": 32, "project": 60, "put": 60, "unpack": 60}

NN = (((1,), (0,)), ((), ()))
NT = (((1,), (1,)), ((), ()))
TN = (((0,), (0,)), ((), ()))


def dot(a, b, dims=NN):
    return lax.dot_general(a, b, dims, preferred_element_type=F32)


def call(
    kernel,
    name,
    grid,
    in_specs,
    out_specs,
    out_shape,
    scratch=(),
    flops=0,
    bytes_accessed=0,
    after=(),
):
    vmem = VMEM_MIB[name.split("_")[0]] * 1024 * 1024
    count, more = len(in_specs), len(after)

    def body(info, *refs):
        kernel(info, *refs[:count], *refs[count + more :])

    made = pl.pallas_call(
        body,
        grid_spec=pltpu.PrefetchScalarGridSpec(
            num_scalar_prefetch=1,
            grid=grid,
            in_specs=list(in_specs) + [pl.BlockSpec(memory_space=pl.ANY)] * more,
            out_specs=out_specs,
            scratch_shapes=list(scratch),
        ),
        out_shape=out_shape,
        compiler_params=pltpu.CompilerParams(
            dimension_semantics=("arbitrary",), vmem_limit_bytes=vmem
        ),
        cost_estimate=pl.CostEstimate(
            flops=int(flops), bytes_accessed=int(bytes_accessed), transcendentals=0
        ),
        name=name,
    )
    return lambda *operands: made(*operands, *after)


def per_step(*shape):
    zeros = (0,) * len(shape)
    return pl.BlockSpec((1,) + shape, lambda s, info: (s,) + zeros)


def whole(*shape):
    zeros = (0,) * len(shape)
    return pl.BlockSpec(shape, lambda s, info: zeros, pipeline_mode=pl.Buffered(1))


def kept(*shape):
    zeros = (0,) * len(shape)
    return pl.BlockSpec(shape, lambda s, info: zeros)


def valid_rows(info, slot, block, positions):
    return jnp.clip(info[slot] - block * positions, 0, positions)


def first_bit(count, slots):
    return slots + 1 + count * slots


def together(count, slots):
    return [d for d in range(1, count) if bin(d).count("1") > 1] if count == 4 and slots > 1 else []


def spread_shapes(count, slots):
    joint = together(count, slots)
    return [()] * (slots * (count - len(joint))) + [(slots,)] * len(joint)


def views(refs, count, slots):
    joint = together(count, slots)
    alone = [d for d in range(count) if d not in joint]
    found = {}
    for slot in range(slots):
        for number, distance in enumerate(alone):
            found[slot * count + distance] = refs[slot * len(alone) + number]
        for number, distance in enumerate(joint):
            found[slot * count + distance] = refs[slots * len(alone) + number].at[slot]
    return [found[n] for n in range(count * slots)]


def pick(count, slots, info, in_ref, *refs):
    sems = refs[-1]
    copies = []
    for number, out in enumerate(views(refs[:-1], count, slots)):
        slot, distance = divmod(number, count)
        source = in_ref.at[info[slots + 1 + distance * slots + slot]]
        copies.append(pltpu.make_async_copy(source, out, sems.at[number]))
    for copy in copies:
        copy.start()
    for copy in copies:
        copy.wait()


def put(count, slots, seqs, rows, last, info, *refs):
    out_ref, held, in_sems, out_sems = refs[count:]
    core = info[first_bit(count, slots)]
    for seq in range(seqs):
        place, slot = place_of(info[last + seq], core, count), info[last + seqs + seq]
        for which, row in enumerate(rows):

            @pl.when(place == which)
            def _():
                pltpu.make_async_copy(
                    refs[which].at[row, slot], held.at[seq], in_sems.at[seq]
                ).start()

    copies = [pltpu.make_async_copy(held.at[n], out_ref.at[n], out_sems.at[n]) for n in range(seqs)]
    for seq, copy in enumerate(copies):
        pltpu.make_async_copy(refs[0].at[0, 0], held.at[seq], in_sems.at[seq]).wait()
        copy.start()
    for copy in copies:
        copy.wait()


def rotate(lin, cos, sin, heads, store):
    for head in range(heads):
        low = head * HEAD_DIM
        lead, trail = lin[low : low + HALF], lin[low + HALF : low + HEAD_DIM]
        store(low, (lead * cos - trail * sin).astype(BF16))
        store(low + HALF, (trail * cos + lead * sin).astype(BF16))


def front(positions, count, slots, info, *refs):
    arrays = len(spread_shapes(count, slots))
    x_refs, refs = views(refs[:arrays], count, slots), refs[arrays:]
    gain_ref, wq_ref, wk_t_ref, wv_t_ref, cos_ref, sin_ref = refs[:6]
    all_ref, normed_ref, q_ref, kv_ref, mix_ref, log_ref, stat, acc, x_now = refs[6:]
    slot = pl.program_id(0)
    blk = info[pl.num_programs(0)]
    blocks = lax.div(info[slot] + positions - 1, positions)

    for distance in range(count):
        block = blk ^ distance
        pick_block(x_refs[distance::count], slot, x_now, block < blocks)

        @pl.when(block < blocks)
        def _():
            x = x_now[...].astype(F32)
            all_ref[0, block] = x_now[...]
            normed = (normalised(x)[0] * gain_ref[...]).astype(BF16)
            normed_ref[0, block] = normed
            cos, sin = cos_ref[block], sin_ref[block]

            def store_kv(low, value):
                kv_ref[0, block, low : low + HALF] = value

            rotate(dot(wk_t_ref[...], normed), cos, sin, KV_HEADS, store_kv)
            kv_ref[0, block, KV_WIDTH:] = dot(wv_t_ref[...], normed).astype(BF16)

            def store_q(low, value):
                q_ref[0, block, low : low + HALF] = value

            rotate(dot(wq_ref[...], normed, TN) * (HEAD_DIM**-0.5), cos, sin, HEADS, store_q)

    def visit(block, other, diagonal):
        if diagonal:
            mask = causal_mask(positions, GROUPS)
        lows = [group * HEAD_DIM for group in range(KV_HEADS)]
        keys = [kv_ref[0, other, low : low + HEAD_DIM] for low in lows]
        values = [kv_ref[0, other, KV_WIDTH + low : KV_WIDTH + low + HEAD_DIM] for low in lows]
        asked = [heads_side_by_side(q_ref, block, group) for group in range(KV_HEADS)]
        if not diagonal:
            olds = [stat[group : group + 1] for group in range(KV_HEADS)]
            sums = [stat[KV_HEADS + group : KV_HEADS + group + 1] for group in range(KV_HEADS)]
            accs = [acc[low : low + HEAD_DIM] for low in lows]
        scores = [dot(keys[group], asked[group], TN) for group in range(KV_HEADS)]
        peaks, totals, mixes = [], [], []
        for group in range(KV_HEADS):
            score = scores[group]
            if diagonal:
                score = jnp.where(mask, score, NEGATIVE)
            peak = jnp.max(score, axis=0, keepdims=True)
            if not diagonal:
                peak = jnp.maximum(peak, olds[group])
            weights = jnp.exp(score - peak)
            total = jnp.sum(weights, axis=0, keepdims=True)
            summed = dot(values[group], weights.astype(BF16))
            if not diagonal:
                fade = jnp.exp(olds[group] - peak)
                total = total + sums[group] * fade
                summed = summed + accs[group] * fade
            peaks.append(peak)
            totals.append(total)
            mixes.append(summed)
        for group, low in enumerate(lows):
            stat[group : group + 1] = peaks[group]
            stat[KV_HEADS + group : KV_HEADS + group + 1] = totals[group]
            acc[low : low + HEAD_DIM] = mixes[group]

    def one_block(block, carry):
        visit(block, block, True)

        def one_pair(other, carry):
            visit(block, other, False)
            return carry

        lax.fori_loop(0, block, one_pair, 0)
        log_ref[0, block] = stat[:KV_HEADS] + jnp.log(stat[KV_HEADS:])
        for group in range(KV_HEADS):
            low = group * HEAD_DIM
            share = 1.0 / stat[KV_HEADS + group : KV_HEADS + group + 1]
            mix = (acc[low : low + HEAD_DIM] * share).astype(BF16)
            for place in range(GROUPS):
                row = (group * GROUPS + place) * HEAD_DIM
                mix_ref[0, block, row : row + HEAD_DIM] = mix[
                    :, place * positions : (place + 1) * positions
                ]
        return carry

    lax.fori_loop(0, blocks, one_block, 0)


def causal_mask(positions, copies):
    keys = lax.broadcasted_iota(jnp.int32, (positions, positions), 0)
    queries = lax.broadcasted_iota(jnp.int32, (positions, positions), 1)
    return jnp.concatenate([keys <= queries] * copies, 1)


def heads_side_by_side(ref, block, group):
    first = group * GROUPS * HEAD_DIM
    return jnp.concatenate(
        [ref[0, block, first + p * HEAD_DIM : first + (p + 1) * HEAD_DIM] for p in range(GROUPS)],
        1,
    )


def pieces_of(columns):
    return [(start, min(LANES, columns - start)) for start in range(0, columns, LANES)]


def place_of(distance, core, count):
    if count == 4:
        return distance ^ (3 * (((distance ^ (distance >> 1)) & 1) * core))
    return distance


class Parts:
    def __init__(self, halves, outs, sems, count, blk):
        self.halves, self.outs, self.sems, self.count, self.blk = halves, outs, sems, count, blk
        self.size = halves[0].shape[0] // count
        self.copies = []

    def write(self, row, value):
        done, rows = 0, value.shape[0]
        while done < rows:
            number, inside = divmod(row + done, self.size)
            take = min(self.size - inside, rows - done)
            half, part = divmod(number, self.count)
            place = place_of(part ^ self.blk, half, self.count)
            start = pl.multiple_of(place * self.size + inside, 16)
            self.halves[half][pl.ds(start, take)] = value[done : done + take]
            done += take
            if inside + take == self.size:
                whole_part = pl.ds(pl.multiple_of(place * self.size, 16), self.size)
                copy = pltpu.make_async_copy(
                    self.halves[half].at[whole_part],
                    self.outs[half].at[whole_part],
                    self.sems.at[number],
                )
                copy.start()
                self.copies.append(copy)


def pack_into(parts, row, acc):
    rows, columns = acc.shape
    for start, width in pieces_of(columns):
        part = acc[:, start : start + width].astype(BF16)
        if width < LANES:
            half = rows // 2
            part = jnp.concatenate([part[:half], part[half:]], 1)
        parts.write(row, part)
        row += part.shape[0]
    return row


def gain_rows(acc):
    ones = jnp.ones((16, acc.shape[1]), BF16)
    sums = dot(ones, acc[...].astype(BF16), NT)[:1]
    parts = [sums[:, start : start + width] for start, width in pieces_of(sums.shape[1])]
    short = LANES - parts[-1].shape[1]
    if short:
        parts[-1] = jnp.concatenate([parts[-1], jnp.zeros((1, short), F32)], 1)
    return parts


def pack_all(info, bit_at, count, blk, buffers, outs, sems, accs, last=None):
    def fill(halves, outs):
        parts = Parts(halves, outs, sems, count, blk)
        row = 0
        for acc in accs:
            row = pack_into(parts, row, acc)
        if last is not None:
            parts.write(row, last)
            row += last.shape[0]
        rest = 2 * halves[0].shape[0] - row
        if rest:
            parts.write(row, jnp.zeros((rest, LANES), BF16))
        for copy in parts.copies:
            copy.wait()

    (mine, send), (mine_out, send_out) = buffers, outs
    pl.when(info[bit_at] == 0)(lambda: fill((mine, send), (mine_out, send_out)))
    pl.when(info[bit_at] != 0)(lambda: fill((send, mine), (send_out, mine_out)))


def packed_rows(rows, columns):
    return rows * columns // LANES


def pick_block(refs, distance, out_ref, wanted):
    for which, ref in enumerate(refs):

        @pl.when(jnp.logical_and(wanted, distance == which))
        def _():
            out_ref[...] = ref[...]


def place_groups(count):
    return [[0, 2], [1, 3]] if count == 4 else [[place] for place in range(count)]


def place_block(refs, count, place, value_ref):
    for ref, group in zip(refs, place_groups(count)):
        inside = functools.reduce(jnp.logical_or, [place == member for member in group])

        @pl.when(inside)
        def _():
            ref[0, 0] = value_ref[...]


def normalised(value):
    scaled = lax.rsqrt(jnp.mean(value * value, axis=0, keepdims=True) + EPS)
    return value * scaled, scaled


def norm_back(upstream, gain, normal, scaled):
    inner = upstream * gain
    return scaled * (inner - normal * jnp.mean(inner * normal, axis=0, keepdims=True))


def valid_lanes(rows, positions):
    lane = lax.broadcasted_iota(jnp.int32, (1, positions), 1)
    return (lane < rows).astype(F32)


def feed_forward(positions, chunk, count, slots, info, *refs):
    arrays = 1 + len(spread_shapes(count, slots))
    x_ref, cot_refs, refs = refs[0], views(refs[1:arrays], count, slots), refs[arrays:]
    mix_ref, gain_ref = refs[:2]
    far_weights = refs[2:6]
    groups = len(place_groups(count))
    out_refs, refs = refs[6 : 6 + groups], refs[6 + groups :]
    mid_ref, gattn_ref, delta_ref, mine_ref, send_ref, gain_sum_ref = refs[:6]
    acc_gate, acc_up, acc_down, acc_out, cot_now, out_now = refs[6:12]
    wo_ref, wg_ref, wu_ref, wd_t_ref = refs[12:16]
    buffers, weight_sems, part_sems = refs[16:18], refs[18], refs[19]
    step = pl.program_id(0)
    place, slot = lax.div(step, slots), lax.rem(step, slots)
    distance = place_of(place, info[first_bit(count, slots)], count)
    rows = valid_rows(info, slot, info[slots] ^ distance, positions)
    width = cot_now.shape[0]
    hidden_width = wg_ref.shape[1]

    everything = slice(None)
    pieces = [("first", 0, (everything, everything))]
    for start in range(0, hidden_width, chunk):
        part = slice(start, start + chunk)
        pieces += [(start, number, (everything, part)) for number in (1, 2, 3)]
    fetches = {}
    for number, (when, weight, where) in enumerate(pieces):
        copy = pltpu.make_async_copy(
            far_weights[weight].at[where], refs[12 + weight].at[where], weight_sems.at[number]
        )
        fetches.setdefault(when, []).append(copy)

    @pl.when(step == 0)
    def _():
        for copies in fetches.values():
            for copy in copies:
                copy.start()
        for acc in (acc_gate, acc_up, acc_down, acc_out, gain_sum_ref):
            acc[...] = jnp.zeros_like(acc)

    @pl.when(jnp.logical_and(rows <= 0, step == 0))
    def _():
        for copies in fetches.values():
            for copy in copies:
                copy.wait()

    @pl.when(rows <= 0)
    def _():
        out_now[...] = jnp.zeros_like(out_now)

    pick_block(cot_refs, slot * count + distance, cot_now, rows > 0)

    def work(need):
        need("first")
        valid = valid_lanes(rows, positions)
        mix = mix_ref[0, 0]
        middle = x_ref[0, 0].astype(F32) + dot(wo_ref[...], mix, TN)
        normal, scaled = normalised(middle)
        gain = gain_ref[...]
        normed = (normal * gain).astype(BF16)
        grad_y = cot_now[...].astype(F32) * valid
        grad_low = grad_y.astype(BF16)
        branch = jnp.zeros((width, positions), F32)
        grad_normed = jnp.zeros((width, positions), F32)
        for start in range(0, hidden_width, chunk):
            part = slice(start, start + chunk)
            need(start)
            gate = dot(wg_ref[:, part], normed, TN)
            up = dot(wu_ref[:, part], normed, TN)
            grad_hidden = dot(wd_t_ref[:, part], grad_low, TN)
            sig = 1.0 / (1.0 + jnp.exp(-gate))
            act = gate * sig
            hidden = (act * up).astype(BF16)
            grad_gate = (grad_hidden * up * (sig * (1.0 + gate * (1.0 - sig)))).astype(BF16)
            grad_up = (grad_hidden * act).astype(BF16)
            branch = branch + dot(wd_t_ref[:, part], hidden)
            grad_normed = grad_normed + dot(wg_ref[:, part], grad_gate)
            grad_normed = grad_normed + dot(wu_ref[:, part], grad_up)
            acc_down[:, part] += dot(grad_low, hidden, NT)
            acc_gate[:, part] += dot(normed, grad_gate, NT)
            acc_up[:, part] += dot(normed, grad_up, NT)
        out_now[...] = (valid * (middle + branch)).astype(BF16)
        gain_sum_ref[...] += grad_normed * normal
        grad_middle = grad_y + norm_back(grad_normed, gain, normal, scaled)
        grad_mid_low = grad_middle.astype(BF16)
        mid_ref[0, 0] = grad_mid_low
        acc_out[...] += dot(mix, grad_mid_low, NT)
        grad_attn = dot(wo_ref[...], grad_mid_low).astype(BF16)
        gattn_ref[0, 0] = grad_attn
        product = grad_attn.astype(F32) * mix.astype(F32)
        for head in range(HEADS):
            part = slice(head * HEAD_DIM, (head + 1) * HEAD_DIM)
            group, turn = head // GROUPS, head % GROUPS
            lanes = slice(turn * positions, (turn + 1) * positions)
            delta_ref[0, 0, group : group + 1, lanes] = jnp.sum(
                product[part], axis=0, keepdims=True
            )

    def wait_for(when):
        for copy in fetches[when]:
            copy.wait()

    pl.when(jnp.logical_and(rows > 0, step == 0))(lambda: work(wait_for))
    pl.when(jnp.logical_and(rows > 0, step > 0))(lambda: work(lambda when: None))

    place_block(out_refs, count, place, out_now)

    @pl.when(step == count * slots - 1)
    def _():
        pack_all(
            info,
            first_bit(count, slots),
            count,
            info[slots],
            buffers,
            (mine_ref, send_ref),
            part_sems,
            (acc_gate, acc_up, acc_down, acc_out),
        )


def rotate_back(value, cos, sin, heads):
    parts = []
    for head in range(heads):
        low = head * HEAD_DIM
        lead, trail = value[low : low + HALF], value[low + HALF : low + HEAD_DIM]
        parts += [lead * cos + trail * sin, trail * cos - lead * sin]
    return jnp.concatenate(parts, 0)


def attend_back(positions, count, info, *refs):
    q_ref, kv_ref, gattn_ref, log_ref, delta_ref, cos_ref, sin_ref = refs[:7]
    lin_ref, dq, dkv = refs[7:]
    blocks = lax.div(info[pl.program_id(0)] + positions - 1, positions)

    def visit(block, other, diagonal):
        if diagonal:
            mask = causal_mask(positions, GROUPS)
        lows = [group * HEAD_DIM for group in range(KV_HEADS)]
        keys = [kv_ref[0, other, low : low + HEAD_DIM] for low in lows]
        values = [kv_ref[0, other, KV_WIDTH + low : KV_WIDTH + low + HEAD_DIM] for low in lows]
        asked = [heads_side_by_side(q_ref, block, group) for group in range(KV_HEADS)]
        grads = [heads_side_by_side(gattn_ref, block, group) for group in range(KV_HEADS)]
        logs = [log_ref[0, block, group : group + 1] for group in range(KV_HEADS)]
        deltas = [delta_ref[0, block, group : group + 1] for group in range(KV_HEADS)]
        results = []
        for group in range(KV_HEADS):
            scores = dot(keys[group], asked[group], TN)
            grad_probs = dot(values[group], grads[group], TN)
            probs = jnp.exp(scores - logs[group])
            if diagonal:
                probs = jnp.where(mask, probs, 0.0)
            grad_scores = (probs * (grad_probs - deltas[group])).astype(BF16)
            grad_value = dot(grads[group], probs.astype(BF16), NT)
            grad_query = dot(keys[group], grad_scores)
            grad_key = dot(asked[group], grad_scores, NT)
            results.append((grad_query, grad_key, grad_value))
        for low, (grad_query, grad_key, grad_value) in zip(lows, results):
            rows = slice(low, low + HEAD_DIM)
            more = slice(KV_WIDTH + low, KV_WIDTH + low + HEAD_DIM)
            if diagonal:
                dq[rows] = grad_query
                dkv[other, rows] = grad_key
                dkv[other, more] = grad_value
            else:
                dq[rows] += grad_query
                dkv[other, rows] += grad_key
                dkv[other, more] += grad_value

    def one_block(block, carry):
        visit(block, block, True)

        def one_pair(other, carry):
            visit(block, other, False)
            return carry

        lax.fori_loop(0, block, one_pair, 0)
        grad = jnp.concatenate(
            [
                dq[
                    (head // GROUPS) * HEAD_DIM : (head // GROUPS + 1) * HEAD_DIM,
                    (head % GROUPS) * positions : (head % GROUPS + 1) * positions,
                ]
                for head in range(HEADS)
            ],
            0,
        ) * (HEAD_DIM**-0.5)
        lin = rotate_back(grad, cos_ref[block], sin_ref[block], HEADS)
        lin_ref[0, block, :Q_WIDTH] = lin.astype(BF16)
        return carry

    lax.fori_loop(0, blocks, one_block, 0)

    def one_rotation(block, carry):
        grad = dkv[block]
        rotated = rotate_back(grad[:KV_WIDTH], cos_ref[block], sin_ref[block], KV_HEADS)
        lin_ref[0, block, Q_WIDTH : Q_WIDTH + KV_WIDTH] = rotated.astype(BF16)
        lin_ref[0, block, Q_WIDTH + KV_WIDTH :] = grad[KV_WIDTH:].astype(BF16)
        return carry

    lax.fori_loop(0, blocks, one_rotation, 0)


def project_back(positions, count, slots, info, *refs):
    x_ref, refs = refs[0], refs[1:]
    gain_ref, normed_ref, lin_ref, mid_ref, wq_ref, wk_t_ref, wv_t_ref, other_gain_ref = refs[:8]
    groups = len(place_groups(count))
    out_refs, refs = refs[8 : 8 + groups], refs[8 + groups :]
    mine_ref, send_ref, gain_sum, acc_q, acc_k, acc_v, out_now = refs[:7]
    buffers, part_sems = refs[7:9], refs[9]
    step = pl.program_id(0)
    place, slot = lax.div(step, slots), lax.rem(step, slots)
    distance = place_of(place, info[first_bit(count, slots)], count)
    blk = info[slots]
    rows = valid_rows(info, slot, blk ^ distance, positions)

    @pl.when(step == 0)
    def _():
        for acc in (acc_q, acc_k, acc_v, gain_sum):
            acc[...] = jnp.zeros_like(acc)


    @pl.when(rows <= 0)
    def _():
        out_now[...] = jnp.zeros_like(out_now)

    @pl.when(rows > 0)
    def _():
        lin = lin_ref[0, 0]
        normed = normed_ref[0, 0]
        acc_q[...] += dot(normed, lin[:Q_WIDTH], NT)
        acc_k[...] += dot(lin[Q_WIDTH : Q_WIDTH + KV_WIDTH], normed, NT)
        acc_v[...] += dot(lin[Q_WIDTH + KV_WIDTH :], normed, NT)
        grad_normed = dot(wq_ref[...], lin[:Q_WIDTH])
        grad_normed += dot(wk_t_ref[...], lin[Q_WIDTH : Q_WIDTH + KV_WIDTH], TN)
        grad_normed += dot(wv_t_ref[...], lin[Q_WIDTH + KV_WIDTH :], TN)
        normal, scaled = normalised(x_ref[0, 0].astype(F32))
        gain_sum[...] += grad_normed * normal
        back = norm_back(grad_normed, gain_ref[...], normal, scaled)
        out_now[...] = (mid_ref[0, 0].astype(F32) + back).astype(BF16)

    place_block(out_refs, count, place, out_now)

    @pl.when(step == count * slots - 1)
    def _():
        gains = gain_rows(gain_sum) + gain_rows(other_gain_ref)
        gains.append(jnp.zeros((-len(gains) % 16, LANES), F32))
        gains = jnp.concatenate(gains, 0).astype(BF16)
        pack_all(
            info,
            first_bit(count, slots),
            count,
            blk,
            buffers,
            (mine_ref, send_ref),
            part_sems,
            (acc_q, acc_k, acc_v),
            gains,
        )


def unpack(count, slots, jobs, info, *refs):
    refs = list(refs)
    take = lambda number: [refs.pop(0) for _ in range(number)]
    core, turn = info[first_bit(count, slots)], info[first_bit(count, slots) + 1]
    sources = [take(count), take(count)]
    outs = [take(len(shapes)) for shapes, *_ in jobs]
    gains = [take(2 if gain_width else 0) for _, _, gain_width, _, _ in jobs]
    buffers = take(len(jobs))
    stages = [take(len(shapes)) for shapes, *_ in jobs]
    in_sems, out_sems = take(2)
    arrivals, number = [], 0
    for (_, shares, _, base, size), buffer in zip(jobs, buffers):
        copies = []
        piece = size // shares
        for which in range(2):
            for place in range(count):
                distance = place_of(place, core ^ which, count)
                part = (core ^ which) * count + (info[slots] ^ distance)
                for share in range(shares):
                    moved = share if shares == 1 else turn ^ share
                    start = pl.multiple_of(part * size + moved * piece, 16)
                    copies.append(
                        pltpu.make_async_copy(
                            sources[which][place].at[pl.ds(base + share * piece, piece)],
                            buffer.at[pl.ds(start, piece)],
                            in_sems.at[number],
                        )
                    )
                    number += 1
        arrivals.append(copies)
    for copies in arrivals:
        for copy in copies:
            copy.start()
    leaving, number = [], 0
    for job, (shapes, _, gain_width, _, _) in enumerate(jobs):
        buffer, row = buffers[job], 0
        for copy in arrivals[job]:
            copy.wait()
        for out, stage, (rows, columns) in zip(outs[job], stages[job], shapes):
            for first, width in pieces_of(columns):
                if width == LANES:
                    stage[:, first : first + LANES] = buffer[row : row + rows].astype(F32)
                    row += rows
                else:
                    half = rows // 2
                    part = buffer[row : row + half].astype(F32)
                    stage[:half, first : first + width] = part[:, :width]
                    stage[half:, first : first + width] = part[:, width:]
                    row += half
            copy = pltpu.make_async_copy(stage, out, out_sems.at[number])
            copy.start()
            leaving.append(copy)
            number += 1
        if gain_width:
            sums, line = buffer[row : row + 16].astype(F32), 0
            for ref in gains[job]:
                for first, width in pieces_of(gain_width):
                    ref[first : first + width] = sums[line, :width]
                    line += 1
    for copy in leaving:
        copy.wait()


def added(arrays):
    total = arrays[0].astype(F32)
    for array in arrays[1:]:
        total = total + array.astype(F32)
    return total.astype(BF16)


def bits_of(count):
    return count.bit_length() - 1


def later(value, *others):
    return lax.optimization_barrier((value, others))[0]


class Sum:
    def __init__(self, blk_count, batch_count):
        self.blk_count, self.rest_count = blk_count, batch_count // 2
        self.rest = lax.axis_index("batch") // 2
        self.bits = bits_of(self.rest_count)

    def swap_cores(self, array):
        pairs = [(i, i ^ 1) for i in range(2 * self.rest_count)]
        return lax.ppermute(array, "batch", pairs)

    def over_blk(self, array, distance):
        return lax.ppermute(array, "blk", [(i, i ^ distance) for i in range(self.blk_count)])

    def over_rest(self, array, bit):
        pairs = [(i, i ^ (2 << bit)) for i in range(2 * self.rest_count)]
        return lax.ppermute(array, "batch", pairs)

    def along(self, array, even, odd):
        pairs = []
        for blk in range(self.blk_count):
            for batch in range(2 * self.rest_count):
                to_blk = blk ^ (odd if batch % 2 else even)
                pairs.append(
                    (blk * 2 * self.rest_count + batch, to_blk * 2 * self.rest_count + batch)
                )
        return lax.ppermute(array, ("blk", "batch"), pairs)

    def reversed_rest(self):
        bits = [((self.rest >> k) & 1) << (self.bits - 1 - k) for k in range(self.bits)]
        return functools.reduce(lambda a, b: a | b, bits, jnp.int32(0))

    def parts_of_chip(self, mine, send):
        got = self.swap_cores(send)
        pieces = 2 if self.blk_count == 4 else self.blk_count
        size = mine.shape[0] // pieces
        return [
            added([array[n * size : (n + 1) * size] for array in (mine, got)])
            for n in range(pieces)
        ]

    def first_hop(self, parts):
        if self.blk_count == 4:
            return [parts[0], self.along(parts[1], 2, 1)]
        return [parts[0]] + [self.over_blk(parts[d], d) for d in range(1, self.blk_count)]

    def second_hop(self, arrays):
        if self.blk_count == 4:
            size = arrays[0].shape[0] // 2
            own = added([array[:size] for array in arrays])
            return [own, self.along(added([array[size:] for array in arrays]), 1, 2)]
        return arrays

    def send_half(self, arrays, k):
        half = arrays[0].shape[0] // 2
        side = (self.rest >> k) & 1

        def cut(which):
            return added([lax.dynamic_slice_in_dim(a, which * half, half, 0) for a in arrays])

        return [cut(side), self.over_rest(cut(1 - side), k)]

    def reduce_rest(self, arrays):
        for k in range(self.bits):
            arrays = self.send_half(arrays, k)
        return added(arrays)

    def gather_rest(self, share):
        block = share
        for k in reversed(range(1, self.bits)):
            block = jnp.concatenate([block, self.over_rest(block, k)], 0)
        return block, self.over_rest(block, 0)

    def reduce_rest_small(self, piece):
        for k in range(self.bits):
            piece = added([piece, self.over_rest(piece, k)])
        return piece

    def gather_blk(self, piece):
        if self.blk_count == 4:
            one, two = self.along(piece, 1, 2), self.along(piece, 2, 1)
            own = [piece, one, two, self.along(later(one, two), 2, 1)]
        else:
            own = [piece] + [self.over_blk(piece, d) for d in range(1, self.blk_count)]
        return own, [self.swap_cores(part) for part in own]


def on_device(
    blk_count,
    batch_count,
    hidden_in,
    lengths,
    attn_gain,
    w_query,
    w_key,
    w_value,
    w_output,
    mlp_gain,
    w_gate,
    w_up,
    w_down,
    cotangent,
):
    seqs, positions, width = hidden_in.shape
    ff = w_gate.shape[1]
    count = blk_count
    devices = blk_count * batch_count
    slots = -(-seqs // count)
    wide = GROUPS * positions
    blk = lax.axis_index("blk")
    x_t = jnp.swapaxes(hidden_in, 1, 2)
    cot_t = jnp.swapaxes(cotangent, 1, 2)

    numbers = jnp.arange(seqs, dtype=jnp.int32)
    ahead = (lengths[None, :] > lengths[:, None]) | (
        (lengths[None, :] == lengths[:, None]) & (numbers[None, :] < numbers[:, None])
    )
    rank = jnp.sum(ahead.astype(jnp.int32), 1)
    slot_of, place = rank // count, rank % count
    batch = lax.axis_index("batch")
    owner = jnp.where((slot_of + batch) % 2 == 0, place, count - 1 - place)
    wanted_device = blk ^ jnp.repeat(jnp.arange(count, dtype=jnp.int32), slots)
    wanted_slot = jnp.tile(jnp.arange(slots, dtype=jnp.int32), count)
    match = (
        (owner[None, :] == wanted_device[:, None]) & (slot_of[None, :] == wanted_slot[:, None])
    ).astype(jnp.int32)
    sequence = jnp.sum(match * numbers[None, :], 1)
    own_lengths = jnp.sum(match[:slots] * lengths[None, :], 1)
    total = Sum(blk_count, batch_count)
    info = jnp.concatenate(
        [own_lengths, jnp.stack([blk]), sequence, jnp.stack([batch % 2, total.reversed_rest()])]
        + [owner ^ blk, slot_of]
    ).astype(jnp.int32)
    bit_at = first_bit(count, slots)

    frequency = np.float32(THETA) ** (
        -np.arange(HALF, dtype=np.float32) * np.float32(2.0) / np.float32(HEAD_DIM)
    )
    places = np.arange(count * positions, dtype=np.float32).reshape(count, 1, positions)
    angles = (frequency[None, :, None] * places).astype(np.float32)
    cos_table, sin_table = jnp.asarray(np.cos(angles)), jnp.asarray(np.sin(angles))
    gain_first = attn_gain.astype(F32)[:, None]
    gain_second = mlp_gain.astype(F32)[:, None]
    anywhere = pl.BlockSpec(memory_space=pl.ANY)

    def spread(array, name, after=None):
        picked = call(
            functools.partial(pick, count, slots),
            name,
            (1,),
            [whole(seqs, width, positions)],
            [anywhere] * len(spread_shapes(count, slots)),
            [
                jax.ShapeDtypeStruct(shape + (width, positions), BF16)
                for shape in spread_shapes(count, slots)
            ],
            [pltpu.SemaphoreType.DMA((count * slots,))],
        )(info, array)
        if after is not None:
            picked = later(picked, after)
        joint = together(count, slots)
        alone = [d for d in range(count) if d not in joint]
        got = []
        for slot in range(slots):
            held = min(count, seqs - slot * count)
            for distance in alone:
                if distance == 0:
                    got.append(picked[len(got)])
                    continue
                pairs = []
                for source in range(count):
                    for other in range(batch_count):
                        target = source ^ distance
                        turn = target if (slot + other) % 2 == 0 else count - 1 - target
                        if turn < held:
                            pairs.append(
                                (source * batch_count + other, target * batch_count + other)
                            )
                got.append(lax.ppermute(picked[len(got)], ("blk", "batch"), pairs))
        for distance in joint:
            got.append(total.over_blk(picked[len(got)], distance))
        return got

    def place_at(info, place):
        return place_of(place, info[bit_at], count)

    def first_back(parts):
        if count == 4:
            return [(parts[0], 0), (parts[0], 1)], total.along(parts[1], 1, 2)
        got = [(parts[0], 0)]
        for distance in range(1, count):
            got.append((total.over_blk(parts[distance], distance), 0))
        return got, None

    def second_back(got, came):
        if count == 4:
            sent = jnp.concatenate([got[1][0][1:], came[1:]], 0)
            final = total.along(sent, 2, 1)
            return [got[0], (came, 0), (final, 0), (final, 1)]
        return got

    def collect(got, name):
        last = bit_at + 2

        return call(
            functools.partial(put, count, slots, seqs, [row for _, row in got], last),
            name,
            (1,),
            [anywhere] * count,
            anywhere,
            jax.ShapeDtypeStruct((seqs, width, positions), BF16),
            [pltpu.VMEM((seqs, width, positions), BF16)]
            + [pltpu.SemaphoreType.DMA((seqs,))] * 2,
        )(info, *[array for array, _ in got])

    spread_specs = [whole(*shape, width, positions) for shape in spread_shapes(count, slots)]
    x_moved = spread(x_t, "pick_hidden")
    cot_moved = spread(cot_t, "pick_cotangent")

    table = whole(count, HALF, positions)
    blocks_of = lambda rows: per_step(count, rows, positions)
    unit_flops = 4 * slots * count * positions * positions * HEADS * 256
    dense = 2 * slots * count * positions * width
    x_all, normed, queries, kv, mix, log_total = call(
        functools.partial(front, positions, count, slots),
        "front",
        (slots,),
        spread_specs
        + [whole(width, 1), whole(width, Q_WIDTH)]
        + [whole(KV_WIDTH, width)] * 2
        + [table, table],
        [
            blocks_of(width),
            blocks_of(width),
            blocks_of(Q_WIDTH),
            blocks_of(2 * KV_WIDTH),
            blocks_of(Q_WIDTH),
            per_step(count, KV_HEADS, wide),
        ],
        [
            jax.ShapeDtypeStruct((slots, count, width, positions), BF16),
            jax.ShapeDtypeStruct((slots, count, width, positions), BF16),
            jax.ShapeDtypeStruct((slots, count, Q_WIDTH, positions), BF16),
            jax.ShapeDtypeStruct((slots, count, 2 * KV_WIDTH, positions), BF16),
            jax.ShapeDtypeStruct((slots, count, Q_WIDTH, positions), BF16),
            jax.ShapeDtypeStruct((slots, count, KV_HEADS, wide), F32),
        ],
        [
            pltpu.VMEM((2 * KV_HEADS, wide), F32),
            pltpu.VMEM((KV_WIDTH, wide), F32),
            pltpu.VMEM((width, positions), BF16),
        ],
        flops=dense * 960 + 2 * unit_flops,
    )(
        info,
        *x_moved,
        gain_first,
        w_query,
        w_key.T,
        w_value.T,
        cos_table,
        sin_table,
    )

    first_shapes = [(width, ff), (width, ff), (width, ff), (Q_WIDTH, width)]
    first_rows = sum(packed_rows(*shape) for shape in first_shapes)
    unit = 16 * devices
    first_half = -(-first_rows // unit) * unit // 2

    def leaving(group):
        def where(step, info):
            now, slot = lax.div(step, slots), lax.rem(step, slots)
            row, at = 0, jnp.where(now < group[0], 0, slots - 1)
            for number, member in enumerate(group):
                row = jnp.where(now >= member, number, row)
                at = jnp.where(now == member, slot, at)
            return (row, at, 0, 0)

        return pl.BlockSpec((1, 1, width, positions), where)

    def block_spec(*shape):
        zeros = (0,) * len(shape)

        def where(step, info):
            place = lax.div(step, slots)
            return (lax.rem(step, slots), info[slots] ^ place_at(info, place)) + zeros

        return pl.BlockSpec((1, 1) + shape, where)

    leavings = [leaving(group) for group in place_groups(count)]
    left = [
        jax.ShapeDtypeStruct((len(group), slots, width, positions), BF16)
        for group in place_groups(count)
    ]
    *layer_t, grad_middle, grad_attn, deltas, mine_first, send_first, gain_sum = call(
        functools.partial(feed_forward, positions, 512, count, slots),
        "feed_forward",
        (slots * count,),
        [block_spec(width, positions)]
        + spread_specs
        + [
            block_spec(Q_WIDTH, positions),
            whole(width, 1),
        ]
        + [anywhere] * 4,
        leavings
        + [
            block_spec(width, positions),
            block_spec(Q_WIDTH, positions),
            block_spec(KV_HEADS, wide),
            anywhere,
            anywhere,
            kept(width, positions),
        ],
        left
        + [
            jax.ShapeDtypeStruct((slots, count, width, positions), BF16),
            jax.ShapeDtypeStruct((slots, count, Q_WIDTH, positions), BF16),
            jax.ShapeDtypeStruct((slots, count, KV_HEADS, wide), F32),
            jax.ShapeDtypeStruct((first_half, LANES), BF16),
            jax.ShapeDtypeStruct((first_half, LANES), BF16),
            jax.ShapeDtypeStruct((width, positions), F32),
        ],
        [pltpu.VMEM(shape, F32) for shape in first_shapes]
        + [pltpu.VMEM((width, positions), BF16)] * 2
        + [pltpu.VMEM((Q_WIDTH, width), BF16)]
        + [pltpu.VMEM((width, ff), BF16)] * 3
        + [pltpu.VMEM((first_half, LANES), BF16)] * 2
        + [
            pltpu.SemaphoreType.DMA((1 + 3 * (ff // 512),)),
            pltpu.SemaphoreType.DMA((2 * count,)),
        ],
        flops=9 * dense * ff,
    )(
        info,
        x_all,
        *cot_moved,
        mix,
        gain_second,
        w_output,
        w_gate,
        w_up,
        w_down.T,
    )

    parts_first = total.parts_of_chip(mine_first, send_first)

    second_shapes = [(width, Q_WIDTH), (KV_WIDTH, width), (KV_WIDTH, width)]
    second_rows = sum(packed_rows(*shape) for shape in second_shapes)
    second_rows += -(-2 * len(pieces_of(width)) // 16) * 16
    second_half = -(-second_rows // unit) * unit // 2
    lin_width = Q_WIDTH + 2 * KV_WIDTH
    grad_lin = call(
        functools.partial(attend_back, positions, count),
        "attend_back",
        (slots,),
        [
            blocks_of(Q_WIDTH),
            blocks_of(2 * KV_WIDTH),
            blocks_of(Q_WIDTH),
            per_step(count, KV_HEADS, wide),
            per_step(count, KV_HEADS, wide),
            table,
            table,
        ],
        blocks_of(lin_width),
        jax.ShapeDtypeStruct((slots, count, lin_width, positions), BF16),
        [
            pltpu.VMEM((KV_WIDTH, wide), F32),
            pltpu.VMEM((count, 2 * KV_WIDTH, positions), F32),
        ],
        flops=5 * unit_flops,
        after=[parts_first[0]],
    )(info, queries, kv, grad_attn, log_total, deltas, cos_table, sin_table)

    layer_got, layer_came = first_back(layer_t)
    hop_first = total.first_hop(parts_first)
    hop_first, layer_came = later((hop_first, layer_came), grad_lin)
    hop_first = total.second_hop(hop_first)
    layer_got = second_back(layer_got, layer_came)

    *grad_in_t, mine_second, send_second = call(
        functools.partial(project_back, positions, count, slots),
        "project_back",
        (slots * count,),
        [
            block_spec(width, positions),
            whole(width, 1),
            block_spec(width, positions),
            block_spec(lin_width, positions),
            block_spec(width, positions),
            whole(width, Q_WIDTH),
            whole(KV_WIDTH, width),
            whole(KV_WIDTH, width),
            whole(width, positions),
        ],
        leavings + [anywhere, anywhere],
        left
        + [
            jax.ShapeDtypeStruct((second_half, LANES), BF16),
            jax.ShapeDtypeStruct((second_half, LANES), BF16),
        ],
        [
            pltpu.VMEM((width, positions), F32),
            pltpu.VMEM((width, Q_WIDTH), F32),
            pltpu.VMEM((KV_WIDTH, width), F32),
            pltpu.VMEM((KV_WIDTH, width), F32),
        ]
        + [pltpu.VMEM((width, positions), BF16)]
        + [pltpu.VMEM((second_half, LANES), BF16)] * 2
        + [pltpu.SemaphoreType.DMA((2 * count,))],
        flops=2 * dense * 960,
        after=[hop_first[0]],
    )(
        info,
        x_all,
        gain_first,
        normed,
        grad_lin,
        grad_middle,
        w_query,
        w_key.T,
        w_value.T,
        gain_sum,
    )
    def tied(got, *others):
        return [(later(array, *others), row) for array, row in got]

    arrays = [array for array, _ in layer_got]
    hop_first, arrays = later((hop_first, arrays), mine_second)
    half_first = total.send_half(hop_first, 0)
    arrays, send_second, grad_in_t = later((arrays, send_second, grad_in_t), half_first[0])
    layer_got = [(array, row) for array, (_, row) in zip(arrays, layer_got)]
    layer_out = collect(layer_got, "put_layer")
    grad_got, grad_came = first_back(grad_in_t)
    half_first = later(half_first, layer_out)
    for k in range(1, total.bits):
        half_first = total.send_half(half_first, k)
    grad_got = second_back(grad_got, grad_came)
    parts_second = total.parts_of_chip(mine_second, send_second)
    piece_second = added(total.second_hop(total.first_hop(parts_second)))
    share = added(half_first)
    block, came = total.gather_rest(share)
    grad_in = collect(tied(grad_got, block), "put_grad")
    piece_second = total.reduce_rest_small(piece_second)
    size_first, size_second = 2 * block.shape[0], piece_second.shape[0]
    piece = jnp.concatenate([block, later(came, grad_in), piece_second], 0)
    own, other = total.gather_blk(piece)
    shares = batch_count // 2
    jobs = [
        (second_shapes, 1, width, size_first, size_second),
        (first_shapes, shares, 0, 0, size_first),
    ]
    results = second_shapes + first_shapes
    g_query, g_key_t, g_value_t, g_gate, g_up, g_down_t, g_out, gain_one, gain_two = call(
        functools.partial(unpack, count, slots, jobs),
        "unpack",
        (1,),
        [anywhere] * (2 * count),
        [anywhere] * len(results) + [kept(width)] * 2,
        [jax.ShapeDtypeStruct(shape, F32) for shape in results]
        + [jax.ShapeDtypeStruct((width,), F32)] * 2,
        [
            pltpu.VMEM((2 * count * size_second, LANES), BF16),
            pltpu.VMEM((2 * count * size_first, LANES), BF16),
        ]
        + [pltpu.VMEM(shape, F32) for shape in results]
        + [
            pltpu.SemaphoreType.DMA((2 * count * (1 + shares),)),
            pltpu.SemaphoreType.DMA((len(results),)),
        ],
        bytes_accessed=12 * count * size_first * LANES,
    )(info, *own, *other)
    return (
        jnp.swapaxes(layer_out, 1, 2),
        jnp.swapaxes(grad_in, 1, 2),
        gain_one,
        g_query,
        g_key_t.T,
        g_value_t.T,
        g_out,
        gain_two,
        g_gate,
        g_up,
        g_down_t.T,
    )


def solution(mesh):
    rows = P("batch", "blk", None)
    return jax.shard_map(
        functools.partial(on_device, mesh.shape["blk"], mesh.shape["batch"]),
        mesh=mesh,
        in_specs=(rows, P("batch")) + (P(),) * 9 + (rows,),
        out_specs=(rows, rows) + (P(),) * 9,
        check_vma=False,
    )
```
